512 devices in a mesh: ja: 128 (over z, y, core), ia: 4 (over x).
Axes of the slice: x: 4, y: 8, z: 8, core: 2. Of those that a mesh axis runs over, the one named last changes fastest.
Arguments:
- positions: float32 [3, 131072], P(None, 'ja'), may hold values from -1 to 1
- velocities: float32 [3, 131072], P(None, 'ja'), may hold values from -3 to 3
- accels: float32 [3, 131072], P(None, 'ja'), may hold values from -3 to 3
- jerks: float32 [3, 131072], P(None, 'ja'), may hold values from -6 to 6
- masses: float32 [131072], P('ja'), may hold values from 2.2888185e-06 to 2.2888184e-05
- last_time: float32 [131072], P('ja'), may hold values from -0.25 to 0
- active: int32 [2, 4096], replicated, may hold values from 0 to 131071, as said below
Outputs:
- new_positions: float32 [3, 131072], P(None, 'ja')
- new_velocities: float32 [3, 131072], P(None, 'ja')
- new_accels: float32 [3, 131072], P(None, 'ja')
- new_jerks: float32 [3, 131072], P(None, 'ja')
- new_times: float32 [131072], P('ja')
- active_state: float32 [2, 12, 4096], replicated
The draws below stay inside these ranges and needn't reach their ends.
Inputs may be any that keep to these rules, and one draw needn't show every extreme that they name: `active`: each row lists 4096 distinct star indices and names both star 0 and star 131072 - 1.
All inputs are finite; a program needn't handle non-finite values.
Results may differ from the reference program's by a relative error of at most 0.0001.
Values sent between devices are 32-bit elements; how exact they have to be, the bound alone decides.
A program may use at most 64 MiB of HBM per device.

```python
import math
import jax
import jax.numpy as jnp
from jax import lax

NSTARS = 131072
ACTIVE = 4096


def draw_active(key, part):
    key = jax.random.fold_in(key, 11)
    rows_out = []
    for section_num in range(2):
        section_key = jax.random.fold_in(key, section_num)
        inner = jax.random.permutation(jax.random.fold_in(section_key, 1), NSTARS - 2)[:ACTIVE - 2] + 1
        ends = jnp.array([0, NSTARS - 1], dtype=jnp.int32)
        combined = jnp.concatenate([ends, inner.astype(jnp.int32)])
        mixing = jax.random.permutation(jax.random.fold_in(section_key, 2), ACTIVE)
        rows_out.append(combined[mixing])
    return jnp.stack(rows_out).astype(jnp.int32)


def level_of(stream_key, shape, shards, low, largest):
    def one(axis_at, shards_of):
        steps = jax.random.uniform(jax.random.fold_in(jax.random.fold_in(stream_key, 6), axis_at), (shards_of,), jnp.float32, low / len(shards), largest / len(shards))
        return jnp.repeat(jnp.exp(steps), shape[axis_at] // shards_of).reshape((-1,) + (1,) * (len(shape) - axis_at - 1))

    factor_of = one(*shards[0])
    for cut in shards[1:]:
        factor_of = factor_of * one(*cut)
    return factor_of


def scatter_about(key, extent, spread, most, cuts=(), kind=jnp.bfloat16):
    level = level_of(key, extent, cuts, -0.22, 0.18) if cuts else 1.0
    values = jax.random.normal(key, extent, jnp.float32) * spread * level
    return jnp.minimum(jnp.maximum(values, -most), most).astype(kind)


def setup_inputs(seed: int = 0) -> dict:
    key_list = jax.random.split(jax.random.key(seed), 8)
    return {
        "positions": jnp.clip(jax.random.uniform(key_list[0], (3, NSTARS), jnp.float32, -1.0, 1.0) * level_of(key_list[0], (3, NSTARS), ((1, 128),), -0.4, 0.0), -1.0, 1.0),
        "velocities": scatter_about(key_list[1], (3, NSTARS), 0.5, 3.0, ((1, 128),), jnp.float32),
        "accels": scatter_about(key_list[2], (3, NSTARS), 0.5, 3.0, ((1, 128),), jnp.float32),
        "jerks": scatter_about(key_list[3], (3, NSTARS), 1.0, 6.0, ((1, 128),), jnp.float32),
        "masses": jnp.clip(jnp.exp(math.log(2.288818359375e-05) - 2.3025851 * jax.random.uniform(key_list[4], (NSTARS,), jnp.float32) ** level_of(key_list[4], (NSTARS,), ((0, 128),), -0.2, 0.2)), 2.28881845032447e-06, 2.288818359375e-05),
        "last_time": jnp.clip(-0.25 + 0.25 * jax.random.uniform(key_list[5], (NSTARS,), jnp.float32) ** level_of(key_list[5], (NSTARS,), ((0, 128),), -0.2, 0.2), -0.25, 0.0),
        "active": draw_active(jax.random.fold_in(key_list[7], 71), 0),
    }


step_length = 0.0625
soft_sq = 0.0025

def predict(positions, velocities, accels, jerks, elapsed):
    pred_pos = positions + elapsed * (velocities + elapsed * (accels / 2.0 + elapsed * jerks / 6.0))
    pred_vel = velocities + elapsed * (accels + elapsed * jerks / 2.0)
    return (pred_pos, pred_vel)

def pair_sums(act_pos, act_vel, field_pos, field_vel, field_mass):
    sep_pos = field_pos[:, None, :] - act_pos[:, :, None]
    sep_vel = field_vel[:, None, :] - act_vel[:, :, None]
    dist_sq = soft_sq + lax.optimization_barrier(jnp.sum(sep_pos * sep_pos, axis=0))
    inv_dist = 1.0 / jnp.sqrt(dist_sq)
    weight = field_mass[None, :] * inv_dist * inv_dist * inv_dist
    radial = 3.0 * lax.optimization_barrier(jnp.sum(sep_pos * sep_vel, axis=0)) / dist_sq
    acc_sum = lax.optimization_barrier(jnp.sum(sep_pos * weight[None], axis=-1))
    jerk_sum = lax.optimization_barrier(jnp.sum((sep_vel - radial[None] * sep_pos) * weight[None], axis=-1))
    return (acc_sum, jerk_sum)

def all_forces(act_pos, act_vel, field_pos, field_vel, field_mass):
    act_block = math.gcd(act_pos.shape[1], 512)
    field_block = math.gcd(field_pos.shape[1], 4096)
    act_count = act_pos.shape[1] // act_block
    field_count = field_pos.shape[1] // field_block
    act_blocks = (act_pos.reshape(3, act_count, act_block).transpose(1, 0, 2), act_vel.reshape(3, act_count, act_block).transpose(1, 0, 2))
    field_blocks = (field_pos.reshape(3, field_count, field_block).transpose(1, 0, 2), field_vel.reshape(3, field_count, field_block).transpose(1, 0, 2), field_mass.reshape(field_count, field_block))

    def one_block(pieces):
        block_pos, block_vel = pieces

        def visit(carry, field_piece):
            acc_sum, jerk_sum = pair_sums(block_pos, block_vel, field_piece[0], field_piece[1], field_piece[2])
            return ((carry[0] + acc_sum, carry[1] + jerk_sum), None)
        start = (jnp.zeros_like(block_pos), jnp.zeros_like(block_pos))
        totals, unused = lax.scan(visit, start, field_blocks)
        return jnp.concatenate([totals[0], totals[1]], axis=0)
    result = lax.map(one_block, act_blocks)
    return result.transpose(1, 0, 2).reshape(6, -1)

def correct(packet, forces):
    pred_pos = packet[0:3]
    pred_vel = packet[3:6]
    old_acc = packet[6:9]
    old_jerk = packet[9:12]
    elapsed = packet[12:13]
    new_acc = forces[0:3]
    new_jerk = forces[3:6]
    elapsed_sq = elapsed * elapsed
    acc_diff = old_acc - new_acc
    snap_coef = (-6.0 * acc_diff - elapsed * (4.0 * old_jerk + 2.0 * new_jerk)) / elapsed_sq
    crackle = (12.0 * acc_diff + 6.0 * elapsed * (old_jerk + new_jerk)) / (elapsed_sq * elapsed)
    new_pos = pred_pos + elapsed_sq * elapsed_sq / 24.0 * snap_coef + elapsed_sq * elapsed_sq * elapsed / 120.0 * crackle
    new_vel = pred_vel + elapsed_sq * elapsed / 6.0 * snap_coef + elapsed_sq * elapsed_sq / 24.0 * crackle
    return jnp.concatenate([new_pos, new_vel, new_acc, new_jerk], axis=0)

def reference(positions, velocities, accels, jerks, masses, last_time, active):
    states = []
    for section_num in range(2):
        time_now = step_length * (section_num + 1)
        elapsed = time_now - last_time
        pred_pos, pred_vel = predict(positions, velocities, accels, jerks, elapsed)
        packet = jnp.concatenate([pred_pos, pred_vel, accels, jerks, elapsed[None]], axis=0)
        chosen = active[section_num].astype(jnp.int32)
        act_rows = jnp.take(packet, chosen, axis=1)
        forces = all_forces(act_rows[0:3], act_rows[3:6], pred_pos, pred_vel, masses)
        fresh_rows = correct(act_rows, forces)
        states.append(fresh_rows)
        positions = positions.at[:, chosen].set(fresh_rows[0:3])
        velocities = velocities.at[:, chosen].set(fresh_rows[3:6])
        accels = accels.at[:, chosen].set(fresh_rows[6:9])
        jerks = jerks.at[:, chosen].set(fresh_rows[9:12])
        last_time = last_time.at[chosen].set(jnp.zeros_like(fresh_rows[0]) + time_now)
    return (positions, velocities, accels, jerks, last_time, jnp.stack(states))
```

```python
import functools

import jax
import jax.numpy as jnp
from jax import lax
from jax.experimental import pallas as pl
from jax.experimental.pallas import tpu as pltpu
from jax.sharding import PartitionSpec as P

MESH = pl.DeviceIdType.MESH
F32 = jnp.float32
BF16 = jnp.bfloat16
STEP = 0.0625
SOFT_SQ = 0.0025
LANES = 128
HALF = 64
CORES = 2
RINGS = {"z": 8, "y": 8, "x": 4}


def split3(value):
    first = value.astype(BF16)
    rest = value - first.astype(F32)
    second = rest.astype(BF16)
    third = (rest - second.astype(F32)).astype(BF16)
    return first, second, third


def dot_nn(left, right):
    return lax.dot_general(left, right, (((1,), (0,)), ((), ())), preferred_element_type=F32)


def dot_nt(left, right):
    return lax.dot_general(left, right, (((1,), (1,)), ((), ())), preferred_element_type=F32)


def exact_nn(left, onehot):
    one, two, three = split3(left)
    return (dot_nn(three, onehot) + dot_nn(two, onehot)) + dot_nn(one, onehot)


def exact_nt(left, onehot):
    one, two, three = split3(left)
    return (dot_nt(three, onehot) + dot_nt(two, onehot)) + dot_nt(one, onehot)


def predict(pos, vel, acc, jerk, elapsed):
    pred_pos = pos + elapsed * (vel + elapsed * (acc / 2.0 + elapsed * jerk / 6.0))
    pred_vel = vel + elapsed * (acc + elapsed * jerk / 2.0)
    return pred_pos, pred_vel


def low_lanes():
    return lax.broadcasted_iota(jnp.int32, (8, LANES), 1) < HALF


def swap(tile):
    return pltpu.roll(tile, HALF, 1)


def pack(low, high):
    return jnp.where(low_lanes(), low, swap(high))


def pair_terms(act, field, sums):
    ax, ay, az, au, av, aw = act
    fx, fy, fz, fu, fv, fw, mass = field
    dx, dy, dz = fx - ax, fy - ay, fz - az
    du, dv, dw = fu - au, fv - av, fw - aw
    dist_sq = (dx * dx + dy * dy) + (dz * dz + SOFT_SQ)
    inv = lax.rsqrt(dist_sq)
    inv_sq = inv * inv
    weight = (mass * inv) * inv_sq
    radial = ((dx * du + dy * dv) + dz * dw) * (3.0 * inv_sq)
    return (
        sums[0] + weight * dx,
        sums[1] + weight * dy,
        sums[2] + weight * dz,
        sums[3] + weight * (du - radial * dx),
        sums[4] + weight * (dv - radial * dy),
        sums[5] + weight * (dw - radial * dz),
    )


def hops(delta, size):
    return min(delta, size - delta)


def kernel(
    sizes,
    pos_in, vel_in, acc_in, jerk_in, mass_in, last_in, act_in,
    pos_out, vel_out, acc_out, jerk_out, time_out, state_out,
    pos_v, vel_v, acc_v, jerk_v, mass_v, last_v, act_v,
    raw, src0, rs_src, rs_dst, pick_src, pick_dst, sum_src, sum_dst,
    field, gath, act_cols, sums_v, corr, low_hot, match, column, scat, fresh,
    in_sem, rs_s, rs_r, pick_s, pick_r, sum_s, sum_r, fz_s, fz_r, fc_s, fc_r,
    ag_s, ag_r, agc_s, agc_r,
):
    zs, ys, xs = sizes
    total = xs * zs * LANES
    quarter = zs * LANES
    ja = lax.axis_index("ja")
    x = lax.axis_index("ia")
    z = lax.div(ja, ys * CORES)
    y = lax.rem(lax.div(ja, CORES), ys)
    c = lax.rem(ja, CORES)

    def device(dz, dy, dc, dx):
        pz = lax.rem(z + dz, zs)
        py = lax.rem(y + dy, ys)
        pc = lax.rem(c + dc, CORES)
        return ((pz * ys + py) * CORES + pc, lax.rem(x + dx, xs))

    zc_list = sorted(
        [(dz, dc) for dz in range(zs) for dc in range(CORES) if (dz, dc) != (0, 0)],
        key=lambda p: -hops(p[0], zs),
    )
    xz_list = sorted(
        [(dz, dx) for dz in range(zs) for dx in range(xs) if (dz, dx) != (0, 0)],
        key=lambda p: -hops(p[0], zs) - hops(p[1], xs),
    )
    y_list = sorted(range(1, ys), key=lambda p: -hops(p, ys))
    z_list = sorted(range(1, zs), key=lambda p: hops(p, zs))
    started = []

    def send(src, dst, ssem, rsem, target):
        copy = pltpu.make_async_remote_copy(
            src_ref=src, dst_ref=dst, send_sem=ssem, recv_sem=rsem,
            device_id=target, device_id_type=MESH,
        )
        copy.start()
        started.append(copy)
        return copy

    loads = [
        pltpu.make_async_copy(a, b, in_sem.at[n])
        for n, (a, b) in enumerate(
            [(pos_in, pos_v), (vel_in, vel_v), (acc_in, acc_v), (jerk_in, jerk_v),
             (mass_in, mass_v), (last_in, last_v), (act_in, act_v)]
        )
    ]
    for load in loads:
        load.start()
    barrier = pltpu.get_barrier_semaphore()
    partners = [(dz, 0, dc, 0) for dz, dc in zc_list]
    partners += [(0, dy, 0, 0) for dy in y_list]
    partners += [(dz, 0, 0, dx) for dz, dx in xz_list if dx != 0]
    for partner in partners:
        pl.semaphore_signal(barrier, inc=1, device_id=device(*partner), device_id_type=MESH)
    for load in loads:
        load.wait()

    for ref, at in ((pos_v, 0), (vel_v, 3), (acc_v, 8), (jerk_v, 11)):
        for comp in range(3):
            for hi in range(8):
                row = (at + comp) * 8 + hi
                raw[row : row + 1, :] = ref[comp : comp + 1, hi * LANES : (hi + 1) * LANES]
    raw[48:56, :] = last_v[...]
    raw[56:64, :] = mass_v[...]

    def value(ref, n):
        return ref[n * 8 : n * 8 + 8, :]

    def predicted(time_now):
        elapsed = time_now - value(raw, 6)
        rows = []
        for comp in range(3):
            rows.append(
                predict(value(raw, comp), value(raw, 3 + comp), value(raw, 8 + comp),
                        value(raw, 11 + comp), elapsed)
            )
        return [r[0] for r in rows] + [r[1] for r in rows], elapsed

    def lay_field(step, rows, mass):
        for n, row in enumerate(rows + [mass]):
            field[step, 0:8, n, :] = row
        field[step, 0:8, 7, :] = jnp.zeros((8, LANES), F32)

    rows0, elapsed0 = predicted(STEP)
    for n, row in enumerate(rows0):
        src0[n * 8 : n * 8 + 8, :] = row
    src0[48:56, :] = elapsed0
    src0[56:112, :] = raw[56:112, :]
    lay_field(0, rows0, value(raw, 7))

    sub = lax.broadcasted_iota(jnp.int32, (LANES, LANES), 0)
    sub8 = lax.broadcasted_iota(jnp.int32, (8, LANES), 0)
    first_star = ja * (8 * LANES)

    def high_hot(step, at):
        local = act_v[step : step + 1, pl.ds(at, LANES)] - first_star
        return jnp.right_shift(local, 7) == sub8

    def low_hot_of(step, at):
        lo = jnp.bitwise_and(act_v[step : step + 1, pl.ds(at, LANES)], LANES - 1)
        return jnp.where(lo == sub, 1.0, 0.0).astype(BF16)

    def pick(step, source):
        pieces = split3(source[...])
        for pz in range(zs):
            at = pl.multiple_of(x * quarter + pz * LANES, LANES)
            hot = low_hot_of(step, at)
            got = (dot_nn(pieces[2], hot) + dot_nn(pieces[1], hot)) + dot_nn(pieces[0], hot)
            own = jnp.where(high_hot(step, at)[None], got.reshape(14, 8, LANES), 0.0)
            rows = jnp.concatenate([jnp.sum(own, axis=1), jnp.zeros((2, LANES), F32)], axis=0)
            low, high = rows[0:8], rows[8:16]
            rs_src[step, pz, 0] = jnp.where(low_lanes(), low, swap(high))
            rs_src[step, pz, 1] = jnp.where(low_lanes(), swap(low), high)

    def scatter_picks(step):
        copies = []
        for dz, dc in zc_list:
            pz, pc = lax.rem(z + dz, zs), lax.rem(c + dc, CORES)
            copies.append(
                send(rs_src.at[step, pz, pc], rs_dst.at[step, dz, dc], rs_s.at[step, dz, dc],
                     rs_r.at[step, dz, dc], device(dz, 0, dc, 0))
            )
        return copies

    def reduce_picks(step, copies):
        for copy in copies:
            copy.wait_recv()
        tile = rs_src[step, z, c]
        for dz, dc in zc_list:
            tile = tile + rs_dst[step, dz, dc]
        pick_src[step] = tile
        return [
            send(pick_src.at[step], pick_dst.at[step, dy], pick_s.at[step, dy],
                 pick_r.at[step, dy], device(0, dy, 0, 0))
            for dy in y_list
        ]

    def picked(step, copies):
        for copy in copies:
            copy.wait_recv()
        tile = pick_src[step]
        for dy in y_list:
            tile = tile + pick_dst[step, dy]
        return tile

    block = 8

    def send_field(step):
        copies = []
        for dz in z_list:
            copies.append(
                send(field.at[step, pl.ds(0, block)], field.at[step, pl.ds(dz * block, block)],
                     fz_s.at[step, dz], fz_r.at[step, dz], device(dz, 0, 0, 0))
            )
        across = [forward(step, 0)]
        return copies, across

    def forward(step, dz):
        return send(
            field.at[step, pl.ds(dz * block, block)],
            field.at[step, pl.ds((zs + dz) * block, block)],
            fc_s.at[step, dz], fc_r.at[step, dz], device(0, 0, 1, 0),
        )

    def pass_on(step, copies, across):
        for dz, copy in zip(z_list, copies):
            copy.wait_recv()
            across.append(forward(step, dz))

    def set_columns(tile):
        wide = jnp.concatenate([tile, jnp.zeros((LANES - 8, LANES), F32)], axis=0).T
        for comp in range(6):
            act_cols[comp] = jnp.broadcast_to(wide[0:HALF, comp : comp + 1], (HALF, LANES))

    def forces(step, begin, end, fresh_start):
        def group(g, _):
            rows = pl.ds(pl.multiple_of(g * 8, 8), 8)
            act = [act_cols[comp, rows, :] for comp in range(6)]

            def tile(t, sums):
                parts = [field[step, t, n : n + 1, :] for n in range(7)]
                return pair_terms(act, parts, sums)

            if fresh_start:
                start = tuple(jnp.zeros((8, LANES), F32) for _ in range(6))
            else:
                start = tuple(sums_v[rows, n * LANES : (n + 1) * LANES] for n in range(6))
            done = lax.fori_loop(begin, end, tile, start, unroll=4)
            for n in range(6):
                sums_v[rows, n * LANES : (n + 1) * LANES] = done[n]
            return 0

        lax.fori_loop(0, 8, group, 0)

    def all_sums(step):
        lane = lax.broadcasted_iota(jnp.int32, (8, 6 * LANES), 1)
        row = lax.broadcasted_iota(jnp.int32, (8, 6 * LANES), 0)
        ones = jnp.where(jnp.right_shift(lane, 7) == row, 1.0, 0.0).astype(BF16)
        one, two, three = split3(sums_v[...])
        rows = (dot_nt(ones, three) + dot_nt(ones, two)) + dot_nt(ones, one)
        sum_src[step] = jnp.concatenate([rows, jnp.zeros((8, HALF), F32)], axis=1)
        return [
            send(sum_src.at[step], sum_dst.at[step, y], sum_s.at[step, dy], sum_r.at[step, y],
                 device(0, dy, 0, 0))
            for dy in y_list
        ]

    def total_sums(step, copies):
        sum_dst[step, y] = sum_src[step]
        for dy in y_list:
            other = lax.rem(y + dy, ys)
            pltpu.make_async_remote_copy(
                src_ref=sum_src.at[step], dst_ref=sum_dst.at[step, other],
                send_sem=sum_s.at[step, dy], recv_sem=sum_r.at[step, other],
                device_id=device(0, dy, 0, 0), device_id_type=MESH,
            ).wait_recv()
        tile = sum_dst[step, 0]
        for n in range(1, ys):
            tile = tile + sum_dst[step, n]
        return tile

    def correct(act, force):
        other = swap(act)
        pred_pos, pred_vel, mass = act[0:3], act[3:6], act[7:8]
        elapsed = jnp.where(low_lanes()[0:1], act[6:7], 1.0)
        old_acc, old_jerk = other[0:3], other[3:6]
        new_acc, new_jerk = force[0:3], force[3:6]
        sq = elapsed * elapsed
        diff = old_acc - new_acc
        snap = (-6.0 * diff - elapsed * (4.0 * old_jerk + 2.0 * new_jerk)) / sq
        crackle = (12.0 * diff + 6.0 * elapsed * (old_jerk + new_jerk)) / (sq * elapsed)
        pos = pred_pos + sq * sq / 24.0 * snap + sq * sq * elapsed / 120.0 * crackle
        vel = pred_vel + sq * elapsed / 6.0 * snap + sq * sq / 24.0 * crackle
        one = jnp.ones((1, LANES), F32)
        low = jnp.concatenate([pos, vel, one, mass], axis=0)
        high = jnp.concatenate([new_acc, new_jerk, one, one], axis=0)
        return pack(low, high)

    def gather_fresh(step, tile):
        gath[step, 0, 0, 0] = tile
        copies = {}
        for dz, dx in xz_list:
            copies[dz, dx] = send(
                gath.at[step, 0, 0, 0], gath.at[step, 0, dz, dx], ag_s.at[step, dz, dx],
                ag_r.at[step, dz, dx], device(dz, 0, 0, dx),
            )
        return copies

    def finish_gather(step, copies):
        across = []
        for dz in [0] + z_list:
            for dx in range(xs):
                if (dz, dx) != (0, 0):
                    copies[dz, dx].wait_recv()
            across.append(
                send(gath.at[step, 0, dz], gath.at[step, 1, dz], agc_s.at[step, dz],
                     agc_r.at[step, dz], device(0, 0, 1, 0))
            )
        for copy in across:
            copy.wait_recv()
        for px in range(xs):
            for pz in range(zs):
                dz, dx = lax.rem(z - pz + zs, zs), lax.rem(x - px + xs, xs)
                tile0 = gath[step, c, dz, dx]
                tile1 = gath[step, 1 - c, dz, dx]
                at = (px * zs + pz) * LANES
                corr[step, 0:8, at : at + LANES] = jnp.where(low_lanes(), tile0, swap(tile1))
                corr[step, 8:16, at : at + LANES] = jnp.where(low_lanes(), swap(tile0), tile1)

    chunks = total // LANES

    def build_low_hot(step):
        def one(n, _):
            at = pl.multiple_of(n * LANES, LANES)
            low_hot[step, :, pl.ds(at, LANES)] = low_hot_of(step, at)
            return 0

        lax.fori_loop(0, chunks, one, 0)

    def hits(step):
        def one(n, seen):
            at = pl.multiple_of(n * LANES, LANES)
            hot = jnp.where(high_hot(step, at), 1.0, 0.0).astype(BF16)
            return seen + dot_nt(hot, low_hot[step, :, pl.ds(at, LANES)])

        return lax.fori_loop(0, chunks, one, jnp.zeros((8, LANES), F32))

    def build_match():
        at = pl.multiple_of(x * quarter + z * LANES, LANES)
        mine = act_v[1:2, pl.ds(at, LANES)].astype(F32)
        column[...] = jnp.broadcast_to(mine, (LANES, LANES)).T
        own = column[pl.ds(pl.multiple_of(c * HALF, HALF), HALF), :]

        def one(n, _):
            at = pl.multiple_of(n * LANES, LANES)
            row = act_v[0:1, pl.ds(at, LANES)].astype(F32)
            match[:, pl.ds(at, LANES)] = jnp.where(own == row, 1.0, 0.0).astype(BF16)
            return 0

        lax.fori_loop(0, chunks, one, 0)

    def place(step, hit):
        names = [0, 1, 2, 3, 4, 5, 8, 9, 10, 11, 12, 13]

        def one(n, done):
            at = pl.multiple_of(n * LANES, LANES)
            mine = high_hot(step, at)
            rows = [
                jnp.where(mine, corr[step, v : v + 1, pl.ds(at, LANES)], 0.0) for v in names
            ]
            left = jnp.concatenate(rows, axis=0)
            return done + exact_nt(left, low_hot[step, :, pl.ds(at, LANES)])

        scat[...] = lax.fori_loop(0, chunks, one, jnp.zeros((96, LANES), F32))
        taken = hit > 0.5
        for n, v in enumerate(names):
            at = v * 8
            raw[at : at + 8, :] = jnp.where(taken, scat[n * 8 : n * 8 + 8, :], raw[at : at + 8, :])
        raw[48:56, :] = jnp.where(taken, STEP * (step + 1), raw[48:56, :])

    def write_state(step):
        state_out[step, 0:6, :] = corr[step, 0:6, :]
        state_out[step, 6:12, :] = corr[step, 8:14, :]

    pick(0, src0)
    pl.semaphore_wait(barrier, len(partners))
    rs0 = scatter_picks(0)
    f0, across0 = send_field(0)
    pick(1, raw)
    rs1 = scatter_picks(1)
    build_low_hot(0)
    hit0 = hits(0)
    fresh[0] = hit0
    rows1, _ = predicted(2 * STEP)
    lay_field(1, rows1, jnp.where(hit0 > 0.5, 0.0, value(raw, 7)))
    ar0 = reduce_picks(0, rs0)
    f1, across1 = send_field(1)
    pass_on(0, f0, across0)
    ar1 = reduce_picks(1, rs1)
    act0 = picked(0, ar0)
    set_columns(act0)
    forces(0, 0, zs * block, True)
    for copy in across0:
        copy.wait_recv()
    forces(0, zs * block, 2 * zs * block, False)
    s0 = all_sums(0)
    pass_on(1, f1, across1)
    act1_raw = picked(1, ar1)
    build_match()
    force0 = total_sums(0, s0)
    fresh0 = gather_fresh(0, correct(act0, force0))
    build_low_hot(1)
    fresh[1] = hits(1)
    for copy in across1:
        copy.wait_recv()
    finish_gather(0, fresh0)

    extra = total // ys
    for n in range(extra // LANES):
        at = pl.multiple_of(y * extra + n * LANES, LANES)
        low = corr[0, 0:8, pl.ds(at, LANES)]
        high = corr[0, 8:16, pl.ds(at, LANES)]
        new_pos, new_vel = predict(low[0:3], low[3:6], high[0:3], high[3:6], 2 * STEP - STEP)
        field[1, 2 * zs * block + n] = jnp.concatenate(
            [new_pos, new_vel, low[7:8], jnp.zeros((1, LANES), F32)], axis=0
        )
    found = exact_nt(corr[0], match[...])
    found = jnp.concatenate([found, jnp.zeros((16, HALF), F32)], axis=1)
    again = found[14:15] > 0.5
    low = jnp.where(again, found[0:8], act1_raw)
    high = jnp.where(again, found[8:16], swap(act1_raw))
    last = jnp.where(again, STEP, act1_raw[6:7])
    elapsed1 = 2 * STEP - last
    pos1, vel1 = predict(low[0:3], low[3:6], high[0:3], high[3:6], elapsed1)
    act1 = pack(jnp.concatenate([pos1, vel1, elapsed1, low[7:8]], axis=0), high)
    set_columns(act1)
    forces(1, 0, 2 * zs * block + extra // LANES, True)
    s1 = all_sums(1)
    place(0, fresh[0])
    write_state(0)
    force1 = total_sums(1, s1)
    fresh1 = gather_fresh(1, correct(act1, force1))
    finish_gather(1, fresh1)
    place(1, fresh[1])
    write_state(1)
    for ref, at in ((pos_out, 0), (vel_out, 3), (acc_out, 8), (jerk_out, 11)):
        for comp in range(3):
            for hi in range(8):
                row = (at + comp) * 8 + hi
                ref[comp : comp + 1, hi * LANES : (hi + 1) * LANES] = raw[row : row + 1, :]
    time_out[...] = raw[48:56, :]
    for copy in started:
        copy.wait_send()


def run(sizes, *args):
    zs, ys, xs = sizes
    total = xs * zs * LANES
    vmem = pltpu.VMEM
    dma = pltpu.SemaphoreType.DMA
    tiles = 2 * zs * 8 + total // ys // LANES
    scratch = [
        vmem((3, 1024), F32), vmem((3, 1024), F32), vmem((3, 1024), F32), vmem((3, 1024), F32),
        vmem((8, LANES), F32), vmem((8, LANES), F32), vmem((2, total), jnp.int32),
        vmem((112, LANES), F32), vmem((112, LANES), F32),
        vmem((2, zs, CORES, 8, LANES), F32), vmem((2, zs, CORES, 8, LANES), F32),
        vmem((2, 8, LANES), F32), vmem((2, ys, 8, LANES), F32),
        vmem((2, 8, LANES), F32), vmem((2, ys, 8, LANES), F32),
        vmem((2, tiles, 8, LANES), F32),
        vmem((2, CORES, zs, xs, 8, LANES), F32),
        vmem((6, HALF, LANES), F32), vmem((HALF, 6 * LANES), F32),
        vmem((2, 16, total), F32), vmem((2, LANES, total), BF16), vmem((HALF, total), BF16),
        vmem((LANES, LANES), F32), vmem((96, LANES), F32), vmem((2, 8, LANES), F32),
        dma((7,)),
        dma((2, zs, CORES)), dma((2, zs, CORES)),
        dma((2, ys)), dma((2, ys)), dma((2, ys)), dma((2, ys)),
        dma((2, zs)), dma((2, zs)), dma((2, zs)), dma((2, zs)),
        dma((2, zs, xs)), dma((2, zs, xs)), dma((2, zs)), dma((2, zs)),
    ]
    flat = jax.ShapeDtypeStruct((3, 1024), F32)
    out_shape = [flat, flat, flat, flat, jax.ShapeDtypeStruct((8, LANES), F32),
                 jax.ShapeDtypeStruct((2, 12, total), F32)]
    return pl.pallas_call(
        functools.partial(kernel, sizes),
        out_shape=out_shape,
        in_specs=[pl.BlockSpec(memory_space=pl.ANY)] * 7,
        out_specs=[pl.BlockSpec(memory_space=pltpu.VMEM)] * 6,
        scratch_shapes=scratch,
        compiler_params=pltpu.CompilerParams(
            collective_id=0, has_side_effects=True, vmem_limit_bytes=48 << 20
        ),
        name="hermite",
    )(*args)


def per_device(sizes, positions, velocities, accels, jerks, masses, last_time, active):
    pos, vel, acc, jerk, times, state = run(
        sizes, positions, velocities, accels, jerks,
        masses.reshape(8, LANES), last_time.reshape(8, LANES), active,
    )
    return pos, vel, acc, jerk, times.reshape(8 * LANES), state


def solution(mesh, sizes=(RINGS["z"], RINGS["y"], RINGS["x"])):
    in_specs = (P(None, "ja"), P(None, "ja"), P(None, "ja"), P(None, "ja"), P("ja"), P("ja"), P())
    out_specs = (P(None, "ja"), P(None, "ja"), P(None, "ja"), P(None, "ja"), P("ja"), P())
    return jax.shard_map(
        functools.partial(per_device, sizes), mesh=mesh, in_specs=in_specs, out_specs=out_specs,
        check_vma=False,
    )
```

```python
import functools

import jax
import jax.numpy as jnp
from jax import lax
from jax.experimental import pallas as pl
from jax.experimental.pallas import tpu as pltpu
from jax.sharding import PartitionSpec as P

MESH = pl.DeviceIdType.MESH
F32 = jnp.float32
BF16 = jnp.bfloat16
STEP = 0.0625
SOFT_SQ = 0.0025
LANES = 128
HALF = 64
CORES = 2
RINGS = {"z": 8, "y": 8, "x": 4}


def split3(value):
    first = value.astype(BF16)
    rest = value - first.astype(F32)
    second = rest.astype(BF16)
    third = (rest - second.astype(F32)).astype(BF16)
    return first, second, third


def dot_nn(left, right):
    return lax.dot_general(left, right, (((1,), (0,)), ((), ())), preferred_element_type=F32)


def dot_nt(left, right):
    return lax.dot_general(left, right, (((1,), (1,)), ((), ())), preferred_element_type=F32)


def exact_nn(left, onehot):
    one, two, three = split3(left)
    return (dot_nn(three, onehot) + dot_nn(two, onehot)) + dot_nn(one, onehot)


def exact_nt(left, onehot):
    one, two, three = split3(left)
    return (dot_nt(three, onehot) + dot_nt(two, onehot)) + dot_nt(one, onehot)


def predict(pos, vel, acc, jerk, elapsed):
    pred_pos = pos + elapsed * (vel + elapsed * (acc / 2.0 + elapsed * jerk / 6.0))
    pred_vel = vel + elapsed * (acc + elapsed * jerk / 2.0)
    return pred_pos, pred_vel


def low_lanes():
    return lax.broadcasted_iota(jnp.int32, (8, LANES), 1) < HALF


def swap(tile):
    return pltpu.roll(tile, HALF, 1)


def pack(low, high):
    return jnp.where(low_lanes(), low, swap(high))


def pair_terms(act, field, sums):
    ax, ay, az, au, av, aw = act
    fx, fy, fz, fu, fv, fw, mass = field
    dx, dy, dz = fx - ax, fy - ay, fz - az
    du, dv, dw = fu - au, fv - av, fw - aw
    dist_sq = (dx * dx + dy * dy) + (dz * dz + SOFT_SQ)
    inv = lax.rsqrt(dist_sq)
    inv_sq = inv * inv
    weight = (mass * inv) * inv_sq
    radial = ((dx * du + dy * dv) + dz * dw) * (3.0 * inv_sq)
    return (
        sums[0] + weight * dx,
        sums[1] + weight * dy,
        sums[2] + weight * dz,
        sums[3] + weight * (du - radial * dx),
        sums[4] + weight * (dv - radial * dy),
        sums[5] + weight * (dw - radial * dz),
    )


def hops(delta, size):
    return min(delta, size - delta)


def kernel(
    sizes,
    pos_in, vel_in, acc_in, jerk_in, mass_in, last_in, act_in,
    pos_out, vel_out, acc_out, jerk_out, time_out, state_out,
    pos_v, vel_v, acc_v, jerk_v, mass_v, last_v, act_v,
    raw, src0, rs_src, rs_dst, pick_src, pick_dst, sum_src, sum_dst,
    field, gath, act_cols, sums_v, corr, low_hot, match, column, scat, fresh, left, state_v, time_v, out_sem,
    in_sem, rs_s, rs_r, pick_s, pick_r, sum_s, sum_r, fz_s, fz_r, fc_s, fc_r,
    ag_s, ag_r, agc_s, agc_r,
):
    zs, ys, xs = sizes
    total = xs * zs * LANES
    quarter = zs * LANES
    ja = lax.axis_index("ja")
    x = lax.axis_index("ia")
    z = lax.div(ja, ys * CORES)
    y = lax.rem(lax.div(ja, CORES), ys)
    c = lax.rem(ja, CORES)

    def device(dz, dy, dc, dx):
        pz = lax.rem(z + dz, zs)
        py = lax.rem(y + dy, ys)
        pc = lax.rem(c + dc, CORES)
        return ((pz * ys + py) * CORES + pc, lax.rem(x + dx, xs))

    zc_list = sorted(
        [(dz, dc) for dz in range(zs) for dc in range(CORES) if (dz, dc) != (0, 0)],
        key=lambda p: -hops(p[0], zs),
    )
    xz_list = sorted(
        [(dz, dx) for dz in range(zs) for dx in range(xs) if (dz, dx) != (0, 0)],
        key=lambda p: -hops(p[0], zs) - hops(p[1], xs),
    )
    y_list = sorted(range(1, ys), key=lambda p: -hops(p, ys))
    z_list = sorted(range(1, zs), key=lambda p: hops(p, zs))
    started = []

    def send(src, dst, ssem, rsem, target):
        copy = pltpu.make_async_remote_copy(
            src_ref=src, dst_ref=dst, send_sem=ssem, recv_sem=rsem,
            device_id=target, device_id_type=MESH,
        )
        copy.start()
        started.append(copy)
        return copy

    loads = [
        pltpu.make_async_copy(a, b, in_sem.at[n])
        for n, (a, b) in enumerate(
            [(pos_in, pos_v), (vel_in, vel_v), (acc_in, acc_v), (jerk_in, jerk_v),
             (mass_in, mass_v), (last_in, last_v), (act_in, act_v)]
        )
    ]
    for load in loads:
        load.start()
    barrier = pltpu.get_barrier_semaphore()
    partners = [(dz, 0, dc, 0) for dz, dc in zc_list]
    partners += [(0, dy, 0, 0) for dy in y_list]
    partners += [(dz, 0, 0, dx) for dz, dx in xz_list if dx != 0]
    for partner in partners:
        pl.semaphore_signal(barrier, inc=1, device_id=device(*partner), device_id_type=MESH)
    for load in loads:
        load.wait()

    for ref, at in ((pos_v, 0), (vel_v, 3), (acc_v, 8), (jerk_v, 11)):
        for comp in range(3):
            for hi in range(8):
                row = (at + comp) * 8 + hi
                raw[row : row + 1, :] = ref[comp : comp + 1, hi * LANES : (hi + 1) * LANES]
    raw[48:56, :] = last_v[...]
    raw[56:64, :] = mass_v[...]

    def value(ref, n):
        return ref[n * 8 : n * 8 + 8, :]

    def predicted(time_now):
        elapsed = time_now - value(raw, 6)
        rows = []
        for comp in range(3):
            rows.append(
                predict(value(raw, comp), value(raw, 3 + comp), value(raw, 8 + comp),
                        value(raw, 11 + comp), elapsed)
            )
        return [r[0] for r in rows] + [r[1] for r in rows], elapsed

    def lay_field(step, rows, mass):
        for n, row in enumerate(rows + [mass]):
            field[step, 0:8, n, :] = row
        field[step, 0:8, 7, :] = jnp.zeros((8, LANES), F32)

    rows0, elapsed0 = predicted(STEP)
    for n, row in enumerate(rows0):
        src0[n * 8 : n * 8 + 8, :] = row
    src0[48:56, :] = elapsed0
    src0[56:112, :] = raw[56:112, :]
    lay_field(0, rows0, value(raw, 7))

    sub = lax.broadcasted_iota(jnp.int32, (LANES, LANES), 0)
    sub8 = lax.broadcasted_iota(jnp.int32, (8, LANES), 0)
    first_star = ja * (8 * LANES)

    def high_hot(step, at):
        local = act_v[step : step + 1, pl.ds(at, LANES)] - first_star
        return jnp.right_shift(local, 7) == sub8

    def low_hot_of(step, at):
        lo = jnp.bitwise_and(act_v[step : step + 1, pl.ds(at, LANES)], LANES - 1)
        return jnp.where(lo == sub, 1.0, 0.0).astype(BF16)

    def pick(step, source):
        pieces = split3(source[...])
        for pz in range(zs):
            at = pl.multiple_of(x * quarter + pz * LANES, LANES)
            hot = low_hot_of(step, at)
            got = (dot_nn(pieces[2], hot) + dot_nn(pieces[1], hot)) + dot_nn(pieces[0], hot)
            own = jnp.where(high_hot(step, at)[None], got.reshape(14, 8, LANES), 0.0)
            rows = jnp.concatenate([jnp.sum(own, axis=1), jnp.zeros((2, LANES), F32)], axis=0)
            low, high = rows[0:8], rows[8:16]
            rs_src[step, pz, 0] = jnp.where(low_lanes(), low, swap(high))
            rs_src[step, pz, 1] = jnp.where(low_lanes(), swap(low), high)

    def scatter_picks(step):
        copies = []
        for dz, dc in zc_list:
            pz, pc = lax.rem(z + dz, zs), lax.rem(c + dc, CORES)
            copies.append(
                send(rs_src.at[step, pz, pc], rs_dst.at[step, dz, dc], rs_s.at[step, dz, dc],
                     rs_r.at[step, dz, dc], device(dz, 0, dc, 0))
            )
        return copies

    def reduce_picks(step, copies):
        for copy in copies:
            copy.wait_recv()
        tile = rs_src[step, z, c]
        for dz, dc in zc_list:
            tile = tile + rs_dst[step, dz, dc]
        pick_src[step] = tile
        return [
            send(pick_src.at[step], pick_dst.at[step, dy], pick_s.at[step, dy],
                 pick_r.at[step, dy], device(0, dy, 0, 0))
            for dy in y_list
        ]

    def picked(step, copies):
        for copy in copies:
            copy.wait_recv()
        tile = pick_src[step]
        for dy in y_list:
            tile = tile + pick_dst[step, dy]
        return tile

    block = 8

    def send_field(step):
        copies = []
        for dz in z_list:
            copies.append(
                send(field.at[step, pl.ds(0, block)], field.at[step, pl.ds(dz * block, block)],
                     fz_s.at[step, dz], fz_r.at[step, dz], device(dz, 0, 0, 0))
            )
        across = [forward(step, 0)]
        return copies, across

    def forward(step, dz):
        return send(
            field.at[step, pl.ds(dz * block, block)],
            field.at[step, pl.ds((zs + dz) * block, block)],
            fc_s.at[step, dz], fc_r.at[step, dz], device(0, 0, 1, 0),
        )

    def pass_on(step, copies, across):
        for dz, copy in zip(z_list, copies):
            copy.wait_recv()
            across.append(forward(step, dz))

    def set_columns(tile):
        wide = jnp.concatenate([tile, jnp.zeros((LANES - 8, LANES), F32)], axis=0).T
        for comp in range(6):
            act_cols[comp] = jnp.broadcast_to(wide[0:HALF, comp : comp + 1], (HALF, LANES))

    def forces(step, begin, end, fresh_start):
        def group(g, _):
            rows = pl.ds(pl.multiple_of(g * 8, 8), 8)
            act = [act_cols[comp, rows, :] for comp in range(6)]

            def tile(t, sums):
                parts = [field[step, t, n : n + 1, :] for n in range(7)]
                return pair_terms(act, parts, sums)

            if fresh_start:
                start = tuple(jnp.zeros((8, LANES), F32) for _ in range(6))
            else:
                start = tuple(sums_v[rows, n * LANES : (n + 1) * LANES] for n in range(6))
            done = lax.fori_loop(begin, end, tile, start, unroll=4)
            for n in range(6):
                sums_v[rows, n * LANES : (n + 1) * LANES] = done[n]
            return 0

        lax.fori_loop(0, 8, group, 0)

    def all_sums(step):
        lane = lax.broadcasted_iota(jnp.int32, (8, 6 * LANES), 1)
        row = lax.broadcasted_iota(jnp.int32, (8, 6 * LANES), 0)
        ones = jnp.where(jnp.right_shift(lane, 7) == row, 1.0, 0.0).astype(BF16)
        one, two, three = split3(sums_v[...])
        rows = (dot_nt(ones, three) + dot_nt(ones, two)) + dot_nt(ones, one)
        sum_src[step] = jnp.concatenate([rows, jnp.zeros((8, HALF), F32)], axis=1)
        return [
            send(sum_src.at[step], sum_dst.at[step, y], sum_s.at[step, dy], sum_r.at[step, y],
                 device(0, dy, 0, 0))
            for dy in y_list
        ]

    def total_sums(step, copies):
        sum_dst[step, y] = sum_src[step]
        for dy in y_list:
            other = lax.rem(y + dy, ys)
            pltpu.make_async_remote_copy(
                src_ref=sum_src.at[step], dst_ref=sum_dst.at[step, other],
                send_sem=sum_s.at[step, dy], recv_sem=sum_r.at[step, other],
                device_id=device(0, dy, 0, 0), device_id_type=MESH,
            ).wait_recv()
        tile = sum_dst[step, 0]
        for n in range(1, ys):
            tile = tile + sum_dst[step, n]
        return tile

    def correct(act, force):
        other = swap(act)
        pred_pos, pred_vel, mass = act[0:3], act[3:6], act[7:8]
        elapsed = jnp.where(low_lanes()[0:1], act[6:7], 1.0)
        old_acc, old_jerk = other[0:3], other[3:6]
        new_acc, new_jerk = force[0:3], force[3:6]
        sq = elapsed * elapsed
        diff = old_acc - new_acc
        snap = (-6.0 * diff - elapsed * (4.0 * old_jerk + 2.0 * new_jerk)) / sq
        crackle = (12.0 * diff + 6.0 * elapsed * (old_jerk + new_jerk)) / (sq * elapsed)
        pos = pred_pos + sq * sq / 24.0 * snap + sq * sq * elapsed / 120.0 * crackle
        vel = pred_vel + sq * elapsed / 6.0 * snap + sq * sq / 24.0 * crackle
        one = jnp.ones((1, LANES), F32)
        low = jnp.concatenate([pos, vel, one, mass], axis=0)
        high = jnp.concatenate([new_acc, new_jerk, one, one], axis=0)
        return pack(low, high)

    def gather_fresh(step, tile):
        gath[step, 0, 0, 0] = tile
        copies = {}
        for dz, dx in xz_list:
            copies[dz, dx] = send(
                gath.at[step, 0, 0, 0], gath.at[step, 0, dz, dx], ag_s.at[step, dz, dx],
                ag_r.at[step, dz, dx], device(dz, 0, 0, dx),
            )
        return copies

    def finish_gather(step, copies):
        across = []
        for dz in [0] + z_list:
            for dx in range(xs):
                if (dz, dx) != (0, 0):
                    copies[dz, dx].wait_recv()
            across.append(
                send(gath.at[step, 0, dz], gath.at[step, 1, dz], agc_s.at[step, dz],
                     agc_r.at[step, dz], device(0, 0, 1, 0))
            )
        for copy in across:
            copy.wait_recv()
        for px in range(xs):
            for pz in range(zs):
                dz, dx = lax.rem(z - pz + zs, zs), lax.rem(x - px + xs, xs)
                tile0 = gath[step, c, dz, dx]
                tile1 = gath[step, 1 - c, dz, dx]
                at = (px * zs + pz) * LANES
                corr[step, 0:8, at : at + LANES] = jnp.where(low_lanes(), tile0, swap(tile1))
                corr[step, 8:16, at : at + LANES] = jnp.where(low_lanes(), swap(tile0), tile1)

    chunks = total // LANES
    names = [0, 1, 2, 3, 4, 5, 8, 9, 10, 11, 12, 13]

    def build_low_hot(step):
        def one(n, _):
            at = pl.multiple_of(n * LANES, LANES)
            low_hot[step, :, pl.ds(at, LANES)] = low_hot_of(step, at)
            return 0

        lax.fori_loop(0, chunks, one, 0)

    def hits(step):
        def one(n, _):
            at = pl.multiple_of(n * LANES, LANES)
            hot = jnp.where(high_hot(step, at), 1.0, 0.0)
            left[0:16, pl.ds(at, LANES)] = jnp.concatenate([hot, hot], axis=0).astype(BF16)
            return 0

        lax.fori_loop(0, chunks, one, 0, unroll=2)
        return dot_nt(left[0:16, :], low_hot[step])[0:8]

    def build_match():
        at = pl.multiple_of(x * quarter + z * LANES, LANES)
        mine = act_v[1:2, pl.ds(at, LANES)].astype(F32)
        column[...] = jnp.broadcast_to(mine, (LANES, LANES)).T
        own = column[pl.ds(pl.multiple_of(c * HALF, HALF), HALF), :]

        def one(n, _):
            at = pl.multiple_of(n * LANES, LANES)
            row = act_v[0:1, pl.ds(at, LANES)].astype(F32)
            match[:, pl.ds(at, LANES)] = jnp.where(own == row, 1.0, 0.0).astype(BF16)
            return 0

        lax.fori_loop(0, chunks, one, 0)

    def place(step, hit):
        def one(n, _):
            at = pl.multiple_of(n * LANES, LANES)
            mine = high_hot(step, at)
            pieces = split3(corr[step, :, pl.ds(at, LANES)])
            for p, piece in enumerate(pieces):
                wide = piece.astype(F32)
                rows = [jnp.where(mine, wide[v : v + 1], 0.0) for v in names]
                left[p * 96 : p * 96 + 96, pl.ds(at, LANES)] = jnp.concatenate(rows, axis=0).astype(BF16)
            return 0

        lax.fori_loop(0, chunks, one, 0, unroll=2)
        got = dot_nt(left[...], low_hot[step])
        scat[...] = (got[192:288] + got[96:192]) + got[0:96]
        taken = hit > 0.5
        for n, v in enumerate(names):
            at = v * 8
            raw[at : at + 8, :] = jnp.where(taken, scat[n * 8 : n * 8 + 8, :], raw[at : at + 8, :])
        raw[48:56, :] = jnp.where(taken, STEP * (step + 1), raw[48:56, :])

    def write_state(step):
        for n, v in enumerate(names):
            state_v[n, step : step + 1, :] = corr[step, v : v + 1, :]

    pick(0, src0)
    pl.semaphore_wait(barrier, len(partners))
    rs0 = scatter_picks(0)
    f0, across0 = send_field(0)
    pick(1, raw)
    rs1 = scatter_picks(1)
    build_low_hot(0)
    hit0 = hits(0)
    fresh[0] = hit0
    rows1, _ = predicted(2 * STEP)
    lay_field(1, rows1, jnp.where(hit0 > 0.5, 0.0, value(raw, 7)))
    ar0 = reduce_picks(0, rs0)
    f1, across1 = send_field(1)
    pass_on(0, f0, across0)
    ar1 = reduce_picks(1, rs1)
    act0 = picked(0, ar0)
    set_columns(act0)
    forces(0, 0, zs * block, True)
    for copy in across0:
        copy.wait_recv()
    forces(0, zs * block, 2 * zs * block, False)
    s0 = all_sums(0)
    pass_on(1, f1, across1)
    act1_raw = picked(1, ar1)
    build_match()
    force0 = total_sums(0, s0)
    fresh0 = gather_fresh(0, correct(act0, force0))
    build_low_hot(1)
    fresh[1] = hits(1)
    for copy in across1:
        copy.wait_recv()
    finish_gather(0, fresh0)

    extra = total // ys
    for n in range(extra // LANES):
        at = pl.multiple_of(y * extra + n * LANES, LANES)
        low = corr[0, 0:8, pl.ds(at, LANES)]
        high = corr[0, 8:16, pl.ds(at, LANES)]
        new_pos, new_vel = predict(low[0:3], low[3:6], high[0:3], high[3:6], 2 * STEP - STEP)
        field[1, 2 * zs * block + n] = jnp.concatenate(
            [new_pos, new_vel, low[7:8], jnp.zeros((1, LANES), F32)], axis=0
        )
    found = exact_nt(corr[0], match[...])
    found = jnp.concatenate([found, jnp.zeros((16, HALF), F32)], axis=1)
    again = found[14:15] > 0.5
    low = jnp.where(again, found[0:8], act1_raw)
    high = jnp.where(again, found[8:16], swap(act1_raw))
    last = jnp.where(again, STEP, act1_raw[6:7])
    elapsed1 = 2 * STEP - last
    pos1, vel1 = predict(low[0:3], low[3:6], high[0:3], high[3:6], elapsed1)
    act1 = pack(jnp.concatenate([pos1, vel1, elapsed1, low[7:8]], axis=0), high)
    set_columns(act1)
    forces(1, 0, 2 * zs * block + extra // LANES, True)
    s1 = all_sums(1)
    place(0, fresh[0])
    write_state(0)
    force1 = total_sums(1, s1)
    fresh1 = gather_fresh(1, correct(act1, force1))
    finish_gather(1, fresh1)
    write_state(1)
    stores = [pltpu.make_async_copy(state_v, state_out, out_sem.at[5])]
    stores[0].start()
    place(1, fresh[1])
    for ref, at in ((pos_v, 0), (vel_v, 3), (acc_v, 8), (jerk_v, 11)):
        for comp in range(3):
            for hi in range(8):
                row = (at + comp) * 8 + hi
                ref[comp : comp + 1, hi * LANES : (hi + 1) * LANES] = raw[row : row + 1, :]
    time_v[...] = raw[48:56, :]
    for n, (a, b) in enumerate(
        [(pos_v, pos_out), (vel_v, vel_out), (acc_v, acc_out), (jerk_v, jerk_out), (time_v, time_out)]
    ):
        stores.append(pltpu.make_async_copy(a, b, out_sem.at[n]))
        stores[-1].start()
    for copy in started:
        copy.wait_send()
    for store in stores:
        store.wait()


def hand_on(*refs):
    srcs, dsts, sem = refs[0:6], refs[6:12], refs[12]
    copies = [pltpu.make_async_copy(a, b, sem.at[n]) for n, (a, b) in enumerate(zip(srcs, dsts))]
    for copy in copies:
        copy.start()
    for copy in copies:
        copy.wait()


def run(sizes, *args):
    zs, ys, xs = sizes
    total = xs * zs * LANES
    vmem = pltpu.VMEM
    dma = pltpu.SemaphoreType.DMA
    tiles = 2 * zs * 8 + total // ys // LANES
    scratch = [
        vmem((3, 1024), F32), vmem((3, 1024), F32), vmem((3, 1024), F32), vmem((3, 1024), F32),
        vmem((8, LANES), F32), vmem((8, LANES), F32), vmem((2, total), jnp.int32),
        vmem((112, LANES), F32), vmem((112, LANES), F32),
        vmem((2, zs, CORES, 8, LANES), F32), vmem((2, zs, CORES, 8, LANES), F32),
        vmem((2, 8, LANES), F32), vmem((2, ys, 8, LANES), F32),
        vmem((2, 8, LANES), F32), vmem((2, ys, 8, LANES), F32),
        vmem((2, tiles, 8, LANES), F32),
        vmem((2, CORES, zs, xs, 8, LANES), F32),
        vmem((6, HALF, LANES), F32), vmem((HALF, 6 * LANES), F32),
        vmem((2, 16, total), F32), vmem((2, LANES, total), BF16), vmem((HALF, total), BF16),
        vmem((LANES, LANES), F32), vmem((96, LANES), F32), vmem((2, 8, LANES), F32),
        vmem((288, total), BF16), vmem((12, 2, total), F32), vmem((8, LANES), F32), dma((6,)),
        dma((7,)),
        dma((2, zs, CORES)), dma((2, zs, CORES)),
        dma((2, ys)), dma((2, ys)), dma((2, ys)), dma((2, ys)),
        dma((2, zs)), dma((2, zs)), dma((2, zs)), dma((2, zs)),
        dma((2, zs, xs)), dma((2, zs, xs)), dma((2, zs)), dma((2, zs)),
    ]
    flat = jax.ShapeDtypeStruct((3, 1024), F32)
    out_shape = [flat, flat, flat, flat, jax.ShapeDtypeStruct((8, LANES), F32),
                 jax.ShapeDtypeStruct((12, 2, total), F32)]
    results = pl.pallas_call(
        functools.partial(kernel, sizes),
        out_shape=out_shape,
        in_specs=[pl.BlockSpec(memory_space=pl.ANY)] * 7,
        out_specs=[pl.BlockSpec(memory_space=pl.ANY)] * 6,
        scratch_shapes=scratch,
        compiler_params=pltpu.CompilerParams(
            collective_id=0, has_side_effects=True, vmem_limit_bytes=62 << 20
        ),
        name="hermite",
    )(*args)
    return pl.pallas_call(
        hand_on,
        out_shape=out_shape,
        in_specs=[pl.BlockSpec(memory_space=pl.ANY)] * 6,
        out_specs=[pl.BlockSpec(memory_space=pl.ANY)] * 6,
        scratch_shapes=[dma((6,))],
        compiler_params=pltpu.CompilerParams(vmem_limit_bytes=62 << 20),
        name="finish",
    )(*results)


def per_device(sizes, positions, velocities, accels, jerks, masses, last_time, active):
    pos, vel, acc, jerk, times, state = run(
        sizes, positions, velocities, accels, jerks,
        masses.reshape(8, LANES), last_time.reshape(8, LANES), active,
    )
    return pos, vel, acc, jerk, times.reshape(8 * LANES), state.transpose(1, 0, 2)


def solution(mesh, sizes=(RINGS["z"], RINGS["y"], RINGS["x"])):
    in_specs = (P(None, "ja"), P(None, "ja"), P(None, "ja"), P(None, "ja"), P("ja"), P("ja"), P())
    out_specs = (P(None, "ja"), P(None, "ja"), P(None, "ja"), P(None, "ja"), P("ja"), P())
    return jax.shard_map(
        functools.partial(per_device, sizes), mesh=mesh, in_specs=in_specs, out_specs=out_specs,
        check_vma=False,
    )
```

```python
import functools

import jax
import jax.numpy as jnp
from jax import lax
from jax.experimental import pallas as pl
from jax.experimental.pallas import tpu as pltpu
from jax.sharding import PartitionSpec as P

MESH = pl.DeviceIdType.MESH
F32 = jnp.float32
BF16 = jnp.bfloat16
STEP = 0.0625
SOFT_SQ = 0.0025
LANES = 128
HALF = 64
CORES = 2
RINGS = {"z": 8, "y": 8, "x": 4}


def split3(value):
    first = value.astype(BF16)
    rest = value - first.astype(F32)
    second = rest.astype(BF16)
    third = (rest - second.astype(F32)).astype(BF16)
    return first, second, third


def dot_nn(left, right):
    return lax.dot_general(left, right, (((1,), (0,)), ((), ())), preferred_element_type=F32)


def dot_nt(left, right):
    return lax.dot_general(left, right, (((1,), (1,)), ((), ())), preferred_element_type=F32)


def exact_nn(left, onehot):
    one, two, three = split3(left)
    return (dot_nn(three, onehot) + dot_nn(two, onehot)) + dot_nn(one, onehot)


def exact_nt(left, onehot):
    one, two, three = split3(left)
    return (dot_nt(three, onehot) + dot_nt(two, onehot)) + dot_nt(one, onehot)


def predict(pos, vel, acc, jerk, elapsed):
    pred_pos = pos + elapsed * (vel + elapsed * (acc / 2.0 + elapsed * jerk / 6.0))
    pred_vel = vel + elapsed * (acc + elapsed * jerk / 2.0)
    return pred_pos, pred_vel


def low_lanes():
    return lax.broadcasted_iota(jnp.int32, (8, LANES), 1) < HALF


def swap(tile):
    return pltpu.roll(tile, HALF, 1)


def pack(low, high):
    return jnp.where(low_lanes(), low, swap(high))


def pair_terms(act, field, sums):
    ax, ay, az, au, av, aw = act
    fx, fy, fz, fu, fv, fw, mass = field
    dx, dy, dz = fx - ax, fy - ay, fz - az
    du, dv, dw = fu - au, fv - av, fw - aw
    dist_sq = (dx * dx + dy * dy) + (dz * dz + SOFT_SQ)
    inv = lax.rsqrt(dist_sq)
    inv_sq = inv * inv
    weight = (mass * inv) * inv_sq
    radial = ((dx * du + dy * dv) + dz * dw) * (3.0 * inv_sq)
    return (
        sums[0] + weight * dx,
        sums[1] + weight * dy,
        sums[2] + weight * dz,
        sums[3] + weight * (du - radial * dx),
        sums[4] + weight * (dv - radial * dy),
        sums[5] + weight * (dw - radial * dz),
    )


def hops(delta, size):
    return min(delta, size - delta)


def kernel(
    sizes,
    pos_in, vel_in, acc_in, jerk_in, mass_in, last_in, act_in,
    pos_out, vel_out, acc_out, jerk_out, time_out, state_out,
    pos_v, vel_v, acc_v, jerk_v, mass_v, last_v, act_v,
    raw, src0, rs_src, rs_dst, pick_src, pick_dst, sum_src, sum_dst,
    field, gath, act_cols, sums_v, corr, low_hot, match, column, scat, fresh, left, state_v, time_v, out_sem,
    in_sem, rs_s, rs_r, pick_s, pick_r, sum_s, sum_r, fz_s, fz_r, fc_s, fc_r,
    ag_s, ag_r, agc_s, agc_r,
):
    zs, ys, xs = sizes
    total = xs * zs * LANES
    quarter = zs * LANES
    ja = lax.axis_index("ja")
    x = lax.axis_index("ia")
    z = lax.div(ja, ys * CORES)
    y = lax.rem(lax.div(ja, CORES), ys)
    c = lax.rem(ja, CORES)

    def device(dz, dy, dc, dx):
        pz = lax.rem(z + dz, zs)
        py = lax.rem(y + dy, ys)
        pc = lax.rem(c + dc, CORES)
        return ((pz * ys + py) * CORES + pc, lax.rem(x + dx, xs))

    zc_list = sorted(
        [(dz, dc) for dz in range(zs) for dc in range(CORES) if (dz, dc) != (0, 0)],
        key=lambda p: -hops(p[0], zs),
    )
    xz_list = sorted(
        [(dz, dx) for dz in range(zs) for dx in range(xs) if (dz, dx) != (0, 0)],
        key=lambda p: -hops(p[0], zs) - hops(p[1], xs),
    )
    y_list = sorted(range(1, ys), key=lambda p: -hops(p, ys))
    z_list = sorted(range(1, zs), key=lambda p: hops(p, zs))
    started = []

    def send(src, dst, ssem, rsem, target):
        copy = pltpu.make_async_remote_copy(
            src_ref=src, dst_ref=dst, send_sem=ssem, recv_sem=rsem,
            device_id=target, device_id_type=MESH,
        )
        copy.start()
        started.append(copy)
        return copy

    loads = [
        pltpu.make_async_copy(a, b, in_sem.at[n])
        for n, (a, b) in enumerate(
            [(pos_in, pos_v), (vel_in, vel_v), (acc_in, acc_v), (jerk_in, jerk_v),
             (mass_in, mass_v), (last_in, last_v), (act_in, act_v)]
        )
    ]
    for load in loads:
        load.start()
    barrier = pltpu.get_barrier_semaphore()
    partners = [(dz, 0, dc, 0) for dz, dc in zc_list]
    partners += [(0, dy, 0, 0) for dy in y_list]
    partners += [(dz, 0, 0, dx) for dz, dx in xz_list if dx != 0]
    for partner in partners:
        pl.semaphore_signal(barrier, inc=1, device_id=device(*partner), device_id_type=MESH)
    for load in loads:
        load.wait()

    for ref, at in ((pos_v, 0), (vel_v, 3), (acc_v, 8), (jerk_v, 11)):
        for comp in range(3):
            for hi in range(8):
                row = (at + comp) * 8 + hi
                raw[row : row + 1, :] = ref[comp : comp + 1, hi * LANES : (hi + 1) * LANES]
    raw[48:56, :] = last_v[...]
    raw[56:64, :] = mass_v[...]

    def value(ref, n):
        return ref[n * 8 : n * 8 + 8, :]

    def predicted(time_now):
        elapsed = time_now - value(raw, 6)
        rows = []
        for comp in range(3):
            rows.append(
                predict(value(raw, comp), value(raw, 3 + comp), value(raw, 8 + comp),
                        value(raw, 11 + comp), elapsed)
            )
        return [r[0] for r in rows] + [r[1] for r in rows], elapsed

    def lay_field(step, rows, mass):
        for n, row in enumerate(rows + [mass]):
            field[step, 0:8, n, :] = row
        field[step, 0:8, 7, :] = jnp.zeros((8, LANES), F32)

    rows0, elapsed0 = predicted(STEP)
    for n, row in enumerate(rows0):
        src0[n * 8 : n * 8 + 8, :] = row
    src0[48:56, :] = elapsed0
    src0[56:112, :] = raw[56:112, :]
    lay_field(0, rows0, value(raw, 7))

    sub = lax.broadcasted_iota(jnp.int32, (LANES, LANES), 0)
    sub8 = lax.broadcasted_iota(jnp.int32, (8, LANES), 0)
    first_star = ja * (8 * LANES)

    def high_hot(step, at):
        local = act_v[step : step + 1, pl.ds(at, LANES)] - first_star
        return jnp.right_shift(local, 7) == sub8

    def low_hot_of(step, at):
        lo = jnp.bitwise_and(act_v[step : step + 1, pl.ds(at, LANES)], LANES - 1)
        return jnp.where(lo == sub, 1.0, 0.0).astype(BF16)

    def pick(step, source):
        pieces = split3(source[...])
        for pz in range(zs):
            at = pl.multiple_of(x * quarter + pz * LANES, LANES)
            hot = low_hot_of(step, at)
            got = (dot_nn(pieces[2], hot) + dot_nn(pieces[1], hot)) + dot_nn(pieces[0], hot)
            own = jnp.where(high_hot(step, at)[None], got.reshape(14, 8, LANES), 0.0)
            rows = jnp.concatenate([jnp.sum(own, axis=1), jnp.zeros((2, LANES), F32)], axis=0)
            low, high = rows[0:8], rows[8:16]
            rs_src[step, pz, 0] = jnp.where(low_lanes(), low, swap(high))
            rs_src[step, pz, 1] = jnp.where(low_lanes(), swap(low), high)

    def scatter_picks(step):
        copies = []
        for dz, dc in zc_list:
            pz, pc = lax.rem(z + dz, zs), lax.rem(c + dc, CORES)
            copies.append(
                send(rs_src.at[step, pz, pc], rs_dst.at[step, dz, dc], rs_s.at[step, dz, dc],
                     rs_r.at[step, dz, dc], device(dz, 0, dc, 0))
            )
        return copies

    def reduce_picks(step, copies):
        for copy in copies:
            copy.wait_recv()
        tile = rs_src[step, z, c]
        for dz, dc in zc_list:
            tile = tile + rs_dst[step, dz, dc]
        pick_src[step] = tile
        return [
            send(pick_src.at[step], pick_dst.at[step, dy], pick_s.at[step, dy],
                 pick_r.at[step, dy], device(0, dy, 0, 0))
            for dy in y_list
        ]

    def picked(step, copies):
        for copy in copies:
            copy.wait_recv()
        tile = pick_src[step]
        for dy in y_list:
            tile = tile + pick_dst[step, dy]
        return tile

    block = 8

    def send_field(step):
        copies = []
        for dz in z_list:
            copies.append(
                send(field.at[step, pl.ds(0, block)], field.at[step, pl.ds(dz * block, block)],
                     fz_s.at[step, dz], fz_r.at[step, dz], device(dz, 0, 0, 0))
            )
        across = [forward(step, 0)]
        return copies, across

    def forward(step, dz):
        return send(
            field.at[step, pl.ds(dz * block, block)],
            field.at[step, pl.ds((zs + dz) * block, block)],
            fc_s.at[step, dz], fc_r.at[step, dz], device(0, 0, 1, 0),
        )

    def pass_on(step, copies, across):
        for dz, copy in zip(z_list, copies):
            copy.wait_recv()
            across.append(forward(step, dz))

    def set_columns(tile):
        wide = jnp.concatenate([tile, jnp.zeros((LANES - 8, LANES), F32)], axis=0).T
        for comp in range(6):
            act_cols[comp] = jnp.broadcast_to(wide[0:HALF, comp : comp + 1], (HALF, LANES))

    def forces(step, begin, end, fresh_start):
        def group(g, _):
            rows = pl.ds(pl.multiple_of(g * 8, 8), 8)
            act = [act_cols[comp, rows, :] for comp in range(6)]

            def tile(t, sums):
                parts = [field[step, t, n : n + 1, :] for n in range(7)]
                return pair_terms(act, parts, sums)

            if fresh_start:
                start = tuple(jnp.zeros((8, LANES), F32) for _ in range(6))
            else:
                start = tuple(sums_v[rows, n * LANES : (n + 1) * LANES] for n in range(6))
            done = lax.fori_loop(begin, end, tile, start, unroll=4)
            for n in range(6):
                sums_v[rows, n * LANES : (n + 1) * LANES] = done[n]
            return 0

        lax.fori_loop(0, 8, group, 0)

    def all_sums(step):
        lane = lax.broadcasted_iota(jnp.int32, (8, 6 * LANES), 1)
        row = lax.broadcasted_iota(jnp.int32, (8, 6 * LANES), 0)
        ones = jnp.where(jnp.right_shift(lane, 7) == row, 1.0, 0.0).astype(BF16)
        one, two, three = split3(sums_v[...])
        rows = (dot_nt(ones, three) + dot_nt(ones, two)) + dot_nt(ones, one)
        sum_src[step] = jnp.concatenate([rows, jnp.zeros((8, HALF), F32)], axis=1)
        return [
            send(sum_src.at[step], sum_dst.at[step, y], sum_s.at[step, dy], sum_r.at[step, y],
                 device(0, dy, 0, 0))
            for dy in y_list
        ]

    def total_sums(step, copies):
        sum_dst[step, y] = sum_src[step]
        for dy in y_list:
            other = lax.rem(y + dy, ys)
            pltpu.make_async_remote_copy(
                src_ref=sum_src.at[step], dst_ref=sum_dst.at[step, other],
                send_sem=sum_s.at[step, dy], recv_sem=sum_r.at[step, other],
                device_id=device(0, dy, 0, 0), device_id_type=MESH,
            ).wait_recv()
        tile = sum_dst[step, 0]
        for n in range(1, ys):
            tile = tile + sum_dst[step, n]
        return tile

    def correct(act, force):
        other = swap(act)
        pred_pos, pred_vel, mass = act[0:3], act[3:6], act[7:8]
        elapsed = jnp.where(low_lanes()[0:1], act[6:7], 1.0)
        old_acc, old_jerk = other[0:3], other[3:6]
        new_acc, new_jerk = force[0:3], force[3:6]
        sq = elapsed * elapsed
        diff = old_acc - new_acc
        snap = (-6.0 * diff - elapsed * (4.0 * old_jerk + 2.0 * new_jerk)) / sq
        crackle = (12.0 * diff + 6.0 * elapsed * (old_jerk + new_jerk)) / (sq * elapsed)
        pos = pred_pos + sq * sq / 24.0 * snap + sq * sq * elapsed / 120.0 * crackle
        vel = pred_vel + sq * elapsed / 6.0 * snap + sq * sq / 24.0 * crackle
        one = jnp.ones((1, LANES), F32)
        low = jnp.concatenate([pos, vel, one, mass], axis=0)
        high = jnp.concatenate([new_acc, new_jerk, one, one], axis=0)
        return pack(low, high)

    def gather_fresh(step, tile):
        gath[step, 0, 0, 0] = tile
        copies = {}
        for dz, dx in xz_list:
            copies[dz, dx] = send(
                gath.at[step, 0, 0, 0], gath.at[step, 0, dz, dx], ag_s.at[step, dz, dx],
                ag_r.at[step, dz, dx], device(dz, 0, 0, dx),
            )
        return copies

    def finish_gather(step, copies):
        across = []
        for dz in [0] + z_list:
            for dx in range(xs):
                if (dz, dx) != (0, 0):
                    copies[dz, dx].wait_recv()
            across.append(
                send(gath.at[step, 0, dz], gath.at[step, 1, dz], agc_s.at[step, dz],
                     agc_r.at[step, dz], device(0, 0, 1, 0))
            )
        for copy in across:
            copy.wait_recv()
        for px in range(xs):
            for pz in range(zs):
                dz, dx = lax.rem(z - pz + zs, zs), lax.rem(x - px + xs, xs)
                tile0 = gath[step, c, dz, dx]
                tile1 = gath[step, 1 - c, dz, dx]
                at = (px * zs + pz) * LANES
                corr[step, 0:8, at : at + LANES] = jnp.where(low_lanes(), tile0, swap(tile1))
                corr[step, 8:16, at : at + LANES] = jnp.where(low_lanes(), swap(tile0), tile1)

    chunks = total // LANES
    names = [0, 1, 2, 3, 4, 5, 8, 9, 10, 11, 12, 13]

    def build_low_hot(step):
        def one(n, _):
            at = pl.multiple_of(n * LANES, LANES)
            low_hot[step, :, pl.ds(at, LANES)] = low_hot_of(step, at)
            return 0

        lax.fori_loop(0, chunks, one, 0)

    def hits(step):
        def one(n, _):
            at = pl.multiple_of(n * LANES, LANES)
            hot = jnp.where(high_hot(step, at), 1.0, 0.0)
            left[0:16, pl.ds(at, LANES)] = jnp.concatenate([hot, hot], axis=0).astype(BF16)
            return 0

        lax.fori_loop(0, chunks, one, 0, unroll=2)
        return dot_nt(left[0:16, :], low_hot[step])[0:8]

    def build_match():
        at = pl.multiple_of(x * quarter + z * LANES, LANES)
        mine = act_v[1:2, pl.ds(at, LANES)].astype(F32)
        column[...] = jnp.broadcast_to(mine, (LANES, LANES)).T
        own = column[pl.ds(pl.multiple_of(c * HALF, HALF), HALF), :]

        def one(n, _):
            at = pl.multiple_of(n * LANES, LANES)
            row = act_v[0:1, pl.ds(at, LANES)].astype(F32)
            match[:, pl.ds(at, LANES)] = jnp.where(own == row, 1.0, 0.0).astype(BF16)
            return 0

        lax.fori_loop(0, chunks, one, 0)

    def place(step, hit):
        def one(n, _):
            at = pl.multiple_of(n * LANES, LANES)
            mine = high_hot(step, at)
            pieces = split3(corr[step, :, pl.ds(at, LANES)])
            for p, piece in enumerate(pieces):
                wide = piece.astype(F32)
                rows = [jnp.where(mine, wide[v : v + 1], 0.0) for v in names]
                left[p * 96 : p * 96 + 96, pl.ds(at, LANES)] = jnp.concatenate(rows, axis=0).astype(BF16)
            return 0

        lax.fori_loop(0, chunks, one, 0, unroll=2)
        got = dot_nt(left[...], low_hot[step])
        scat[...] = (got[192:288] + got[96:192]) + got[0:96]
        taken = hit > 0.5
        for n, v in enumerate(names):
            at = v * 8
            raw[at : at + 8, :] = jnp.where(taken, scat[n * 8 : n * 8 + 8, :], raw[at : at + 8, :])
        raw[48:56, :] = jnp.where(taken, STEP * (step + 1), raw[48:56, :])

    def write_state(step):
        for n, v in enumerate(names):
            state_v[n, step : step + 1, :] = corr[step, v : v + 1, :]

    pick(0, src0)
    pl.semaphore_wait(barrier, len(partners))
    rs0 = scatter_picks(0)
    f0, across0 = send_field(0)
    pick(1, raw)
    rs1 = scatter_picks(1)
    build_low_hot(0)
    hit0 = hits(0)
    fresh[0] = hit0
    rows1, _ = predicted(2 * STEP)
    lay_field(1, rows1, jnp.where(hit0 > 0.5, 0.0, value(raw, 7)))
    ar0 = reduce_picks(0, rs0)
    f1, across1 = send_field(1)
    pass_on(0, f0, across0)
    ar1 = reduce_picks(1, rs1)
    act0 = picked(0, ar0)
    set_columns(act0)
    forces(0, 0, zs * block, True)
    for copy in across0:
        copy.wait_recv()
    forces(0, zs * block, 2 * zs * block, False)
    s0 = all_sums(0)
    pass_on(1, f1, across1)
    act1_raw = picked(1, ar1)
    build_match()
    force0 = total_sums(0, s0)
    fresh0 = gather_fresh(0, correct(act0, force0))
    build_low_hot(1)
    fresh[1] = hits(1)
    for copy in across1:
        copy.wait_recv()
    finish_gather(0, fresh0)

    extra = total // ys
    for n in range(extra // LANES):
        at = pl.multiple_of(y * extra + n * LANES, LANES)
        low = corr[0, 0:8, pl.ds(at, LANES)]
        high = corr[0, 8:16, pl.ds(at, LANES)]
        new_pos, new_vel = predict(low[0:3], low[3:6], high[0:3], high[3:6], 2 * STEP - STEP)
        field[1, 2 * zs * block + n] = jnp.concatenate(
            [new_pos, new_vel, low[7:8], jnp.zeros((1, LANES), F32)], axis=0
        )
    found = exact_nt(corr[0], match[...])
    found = jnp.concatenate([found, jnp.zeros((16, HALF), F32)], axis=1)
    again = found[14:15] > 0.5
    low = jnp.where(again, found[0:8], act1_raw)
    high = jnp.where(again, found[8:16], swap(act1_raw))
    last = jnp.where(again, STEP, act1_raw[6:7])
    elapsed1 = 2 * STEP - last
    pos1, vel1 = predict(low[0:3], low[3:6], high[0:3], high[3:6], elapsed1)
    act1 = pack(jnp.concatenate([pos1, vel1, elapsed1, low[7:8]], axis=0), high)
    set_columns(act1)
    forces(1, 0, 2 * zs * block + extra // LANES, True)
    s1 = all_sums(1)
    place(0, fresh[0])
    write_state(0)
    force1 = total_sums(1, s1)
    fresh1 = gather_fresh(1, correct(act1, force1))
    finish_gather(1, fresh1)
    write_state(1)
    stores = [pltpu.make_async_copy(state_v, state_out, out_sem.at[5])]
    stores[0].start()
    place(1, fresh[1])
    for ref, at in ((pos_v, 0), (vel_v, 3), (acc_v, 8), (jerk_v, 11)):
        for comp in range(3):
            for hi in range(8):
                row = (at + comp) * 8 + hi
                ref[comp : comp + 1, hi * LANES : (hi + 1) * LANES] = raw[row : row + 1, :]
    time_v[...] = raw[48:56, :]
    for n, (a, b) in enumerate(
        [(pos_v, pos_out), (vel_v, vel_out), (acc_v, acc_out), (jerk_v, jerk_out), (time_v, time_out)]
    ):
        stores.append(pltpu.make_async_copy(a, b, out_sem.at[n]))
        stores[-1].start()
    for copy in started:
        copy.wait_send()
    for store in stores:
        store.wait()


def hand_on(*refs):
    srcs, dsts, held, sem = refs[0:6], refs[6:12], refs[12:18], refs[18]
    loads = [pltpu.make_async_copy(a, b, sem.at[0, n]) for n, (a, b) in enumerate(zip(srcs, held))]
    stores = [pltpu.make_async_copy(a, b, sem.at[1, n]) for n, (a, b) in enumerate(zip(held, dsts))]
    for load in loads:
        load.start()
    for load, store in zip(loads, stores):
        load.wait()
        store.start()
    for store in stores:
        store.wait()


def run(sizes, *args):
    zs, ys, xs = sizes
    total = xs * zs * LANES
    vmem = pltpu.VMEM
    dma = pltpu.SemaphoreType.DMA
    tiles = 2 * zs * 8 + total // ys // LANES
    scratch = [
        vmem((3, 1024), F32), vmem((3, 1024), F32), vmem((3, 1024), F32), vmem((3, 1024), F32),
        vmem((8, LANES), F32), vmem((8, LANES), F32), vmem((2, total), jnp.int32),
        vmem((112, LANES), F32), vmem((112, LANES), F32),
        vmem((2, zs, CORES, 8, LANES), F32), vmem((2, zs, CORES, 8, LANES), F32),
        vmem((2, 8, LANES), F32), vmem((2, ys, 8, LANES), F32),
        vmem((2, 8, LANES), F32), vmem((2, ys, 8, LANES), F32),
        vmem((2, tiles, 8, LANES), F32),
        vmem((2, CORES, zs, xs, 8, LANES), F32),
        vmem((6, HALF, LANES), F32), vmem((HALF, 6 * LANES), F32),
        vmem((2, 16, total), F32), vmem((2, LANES, total), BF16), vmem((HALF, total), BF16),
        vmem((LANES, LANES), F32), vmem((96, LANES), F32), vmem((2, 8, LANES), F32),
        vmem((288, total), BF16), vmem((12, 2, total), F32), vmem((8, LANES), F32), dma((6,)),
        dma((7,)),
        dma((2, zs, CORES)), dma((2, zs, CORES)),
        dma((2, ys)), dma((2, ys)), dma((2, ys)), dma((2, ys)),
        dma((2, zs)), dma((2, zs)), dma((2, zs)), dma((2, zs)),
        dma((2, zs, xs)), dma((2, zs, xs)), dma((2, zs)), dma((2, zs)),
    ]
    flat = jax.ShapeDtypeStruct((3, 1024), F32)
    out_shape = [flat, flat, flat, flat, jax.ShapeDtypeStruct((8, LANES), F32),
                 jax.ShapeDtypeStruct((12, 2, total), F32)]
    results = pl.pallas_call(
        functools.partial(kernel, sizes),
        out_shape=out_shape,
        in_specs=[pl.BlockSpec(memory_space=pl.ANY)] * 7,
        out_specs=[pl.BlockSpec(memory_space=pl.ANY)] * 6,
        scratch_shapes=scratch,
        compiler_params=pltpu.CompilerParams(
            collective_id=0, has_side_effects=True, vmem_limit_bytes=62 << 20
        ),
        name="hermite",
    )(*args)
    return pl.pallas_call(
        hand_on,
        out_shape=out_shape,
        in_specs=[pl.BlockSpec(memory_space=pl.ANY)] * 6,
        out_specs=[pl.BlockSpec(memory_space=pl.ANY)] * 6,
        scratch_shapes=[vmem(out.shape, F32) for out in out_shape] + [dma((2, 6))],
        compiler_params=pltpu.CompilerParams(vmem_limit_bytes=62 << 20),
        name="finish",
    )(*results)


def per_device(sizes, positions, velocities, accels, jerks, masses, last_time, active):
    pos, vel, acc, jerk, times, state = run(
        sizes, positions, velocities, accels, jerks,
        masses.reshape(8, LANES), last_time.reshape(8, LANES), active,
    )
    return pos, vel, acc, jerk, times.reshape(8 * LANES), state.transpose(1, 0, 2)


def solution(mesh, sizes=(RINGS["z"], RINGS["y"], RINGS["x"])):
    in_specs = (P(None, "ja"), P(None, "ja"), P(None, "ja"), P(None, "ja"), P("ja"), P("ja"), P())
    out_specs = (P(None, "ja"), P(None, "ja"), P(None, "ja"), P(None, "ja"), P("ja"), P())
    return jax.shard_map(
        functools.partial(per_device, sizes), mesh=mesh, in_specs=in_specs, out_specs=out_specs,
        check_vma=False,
    )
```

```python
import functools

import jax
import jax.numpy as jnp
from jax import lax
from jax.experimental import pallas as pl
from jax.experimental.pallas import tpu as pltpu
from jax.sharding import PartitionSpec as P

MESH = pl.DeviceIdType.MESH
F32 = jnp.float32
BF16 = jnp.bfloat16
STEP = 0.0625
SOFT_SQ = 0.0025
LANES = 128
HALF = 64
CORES = 2
RINGS = {"z": 8, "y": 8, "x": 4}


def split3(value):
    first = value.astype(BF16)
    rest = value - first.astype(F32)
    second = rest.astype(BF16)
    third = (rest - second.astype(F32)).astype(BF16)
    return first, second, third


def dot_nn(left, right):
    return lax.dot_general(left, right, (((1,), (0,)), ((), ())), preferred_element_type=F32)


def dot_nt(left, right):
    return lax.dot_general(left, right, (((1,), (1,)), ((), ())), preferred_element_type=F32)


def exact_nn(left, onehot):
    one, two, three = split3(left)
    return (dot_nn(three, onehot) + dot_nn(two, onehot)) + dot_nn(one, onehot)


def exact_nt(left, onehot):
    one, two, three = split3(left)
    return (dot_nt(three, onehot) + dot_nt(two, onehot)) + dot_nt(one, onehot)


def predict(pos, vel, acc, jerk, elapsed):
    pred_pos = pos + elapsed * (vel + elapsed * (acc / 2.0 + elapsed * jerk / 6.0))
    pred_vel = vel + elapsed * (acc + elapsed * jerk / 2.0)
    return pred_pos, pred_vel


def low_lanes():
    return lax.broadcasted_iota(jnp.int32, (8, LANES), 1) < HALF


def swap(tile):
    return pltpu.roll(tile, HALF, 1)


def pack(low, high):
    return jnp.where(low_lanes(), low, swap(high))


def pair_terms(act, field, sums):
    ax, ay, az, au, av, aw = act
    fx, fy, fz, fu, fv, fw, mass = field
    dx, dy, dz = fx - ax, fy - ay, fz - az
    du, dv, dw = fu - au, fv - av, fw - aw
    dist_sq = (dx * dx + dy * dy) + (dz * dz + SOFT_SQ)
    inv = lax.rsqrt(dist_sq)
    inv_sq = inv * inv
    weight = (mass * inv) * inv_sq
    radial = ((dx * du + dy * dv) + dz * dw) * (3.0 * inv_sq)
    return (
        sums[0] + weight * dx,
        sums[1] + weight * dy,
        sums[2] + weight * dz,
        sums[3] + weight * (du - radial * dx),
        sums[4] + weight * (dv - radial * dy),
        sums[5] + weight * (dw - radial * dz),
    )


def hops(delta, size):
    return min(delta, size - delta)


def kernel(
    sizes,
    pos_in, vel_in, acc_in, jerk_in, mass_in, last_in, act_in,
    pos_out, vel_out, acc_out, jerk_out, time_out, state_out,
    pos_v, vel_v, acc_v, jerk_v, mass_v, last_v, act_v,
    raw, src0, rs_src, rs_dst, pick_src, pick_dst, sum_src, sum_dst,
    field, gath, act_cols, sums_v, corr, low_hot, match, column, scat, fresh, left,
    in_sem, rs_s, rs_r, pick_s, pick_r, sum_s, sum_r, fz_s, fz_r, fc_s, fc_r,
    ag_s, ag_r, agc_s, agc_r,
):
    zs, ys, xs = sizes
    total = xs * zs * LANES
    quarter = zs * LANES
    ja = lax.axis_index("ja")
    x = lax.axis_index("ia")
    z = lax.div(ja, ys * CORES)
    y = lax.rem(lax.div(ja, CORES), ys)
    c = lax.rem(ja, CORES)

    def device(dz, dy, dc, dx):
        pz = lax.rem(z + dz, zs)
        py = lax.rem(y + dy, ys)
        pc = lax.rem(c + dc, CORES)
        return ((pz * ys + py) * CORES + pc, lax.rem(x + dx, xs))

    zc_list = sorted(
        [(dz, dc) for dz in range(zs) for dc in range(CORES) if (dz, dc) != (0, 0)],
        key=lambda p: -hops(p[0], zs),
    )
    xz_list = sorted(
        [(dz, dx) for dz in range(zs) for dx in range(xs) if (dz, dx) != (0, 0)],
        key=lambda p: -hops(p[0], zs) - hops(p[1], xs),
    )
    y_list = sorted(range(1, ys), key=lambda p: -hops(p, ys))
    z_list = sorted(range(1, zs), key=lambda p: hops(p, zs))
    started = []

    def send(src, dst, ssem, rsem, target):
        copy = pltpu.make_async_remote_copy(
            src_ref=src, dst_ref=dst, send_sem=ssem, recv_sem=rsem,
            device_id=target, device_id_type=MESH,
        )
        copy.start()
        started.append(copy)
        return copy

    loads = [
        pltpu.make_async_copy(a, b, in_sem.at[n])
        for n, (a, b) in enumerate(
            [(pos_in, pos_v), (vel_in, vel_v), (acc_in, acc_v), (jerk_in, jerk_v),
             (mass_in, mass_v), (last_in, last_v), (act_in, act_v)]
        )
    ]
    for load in loads:
        load.start()
    barrier = pltpu.get_barrier_semaphore()
    partners = [(dz, 0, dc, 0) for dz, dc in zc_list]
    partners += [(0, dy, 0, 0) for dy in y_list]
    partners += [(dz, 0, 0, dx) for dz, dx in xz_list if dx != 0]
    for partner in partners:
        pl.semaphore_signal(barrier, inc=1, device_id=device(*partner), device_id_type=MESH)
    for load in loads:
        load.wait()

    for ref, at in ((pos_v, 0), (vel_v, 3), (acc_v, 8), (jerk_v, 11)):
        for comp in range(3):
            for hi in range(8):
                row = (at + comp) * 8 + hi
                raw[row : row + 1, :] = ref[comp : comp + 1, hi * LANES : (hi + 1) * LANES]
    raw[48:56, :] = last_v[...]
    raw[56:64, :] = mass_v[...]

    def value(ref, n):
        return ref[n * 8 : n * 8 + 8, :]

    def predicted(time_now):
        elapsed = time_now - value(raw, 6)
        rows = []
        for comp in range(3):
            rows.append(
                predict(value(raw, comp), value(raw, 3 + comp), value(raw, 8 + comp),
                        value(raw, 11 + comp), elapsed)
            )
        return [r[0] for r in rows] + [r[1] for r in rows], elapsed

    def lay_field(step, rows, mass):
        for n, row in enumerate(rows + [mass]):
            field[step, 0:8, n, :] = row
        field[step, 0:8, 7, :] = jnp.zeros((8, LANES), F32)

    rows0, elapsed0 = predicted(STEP)
    for n, row in enumerate(rows0):
        src0[n * 8 : n * 8 + 8, :] = row
    src0[48:56, :] = elapsed0
    src0[56:112, :] = raw[56:112, :]
    lay_field(0, rows0, value(raw, 7))

    sub = lax.broadcasted_iota(jnp.int32, (LANES, LANES), 0)
    sub8 = lax.broadcasted_iota(jnp.int32, (8, LANES), 0)
    first_star = ja * (8 * LANES)

    def high_hot(step, at):
        local = act_v[step : step + 1, pl.ds(at, LANES)] - first_star
        return jnp.right_shift(local, 7) == sub8

    def low_hot_of(step, at):
        lo = jnp.bitwise_and(act_v[step : step + 1, pl.ds(at, LANES)], LANES - 1)
        return jnp.where(lo == sub, 1.0, 0.0).astype(BF16)

    def pick(step, source):
        pieces = split3(source[...])
        for pz in range(zs):
            at = pl.multiple_of(x * quarter + pz * LANES, LANES)
            hot = low_hot_of(step, at)
            got = (dot_nn(pieces[2], hot) + dot_nn(pieces[1], hot)) + dot_nn(pieces[0], hot)
            own = jnp.where(high_hot(step, at)[None], got.reshape(14, 8, LANES), 0.0)
            rows = jnp.concatenate([jnp.sum(own, axis=1), jnp.zeros((2, LANES), F32)], axis=0)
            low, high = rows[0:8], rows[8:16]
            rs_src[step, pz, 0] = jnp.where(low_lanes(), low, swap(high))
            rs_src[step, pz, 1] = jnp.where(low_lanes(), swap(low), high)

    def scatter_picks(step):
        copies = []
        for dz, dc in zc_list:
            pz, pc = lax.rem(z + dz, zs), lax.rem(c + dc, CORES)
            copies.append(
                send(rs_src.at[step, pz, pc], rs_dst.at[step, dz, dc], rs_s.at[step, dz, dc],
                     rs_r.at[step, dz, dc], device(dz, 0, dc, 0))
            )
        return copies

    def reduce_picks(step, copies):
        for copy in copies:
            copy.wait_recv()
        tile = rs_src[step, z, c]
        for dz, dc in zc_list:
            tile = tile + rs_dst[step, dz, dc]
        pick_src[step] = tile
        return [
            send(pick_src.at[step], pick_dst.at[step, dy], pick_s.at[step, dy],
                 pick_r.at[step, dy], device(0, dy, 0, 0))
            for dy in y_list
        ]

    def picked(step, copies):
        for copy in copies:
            copy.wait_recv()
        tile = pick_src[step]
        for dy in y_list:
            tile = tile + pick_dst[step, dy]
        return tile

    block = 8

    def send_field(step):
        copies = []
        for dz in z_list:
            copies.append(
                send(field.at[step, pl.ds(0, block)], field.at[step, pl.ds(dz * block, block)],
                     fz_s.at[step, dz], fz_r.at[step, dz], device(dz, 0, 0, 0))
            )
        across = [forward(step, 0)]
        return copies, across

    def forward(step, dz):
        return send(
            field.at[step, pl.ds(dz * block, block)],
            field.at[step, pl.ds((zs + dz) * block, block)],
            fc_s.at[step, dz], fc_r.at[step, dz], device(0, 0, 1, 0),
        )

    def pass_on(step, copies, across):
        for dz, copy in zip(z_list, copies):
            copy.wait_recv()
            across.append(forward(step, dz))

    def set_columns(tile):
        wide = jnp.concatenate([tile, jnp.zeros((LANES - 8, LANES), F32)], axis=0).T
        for comp in range(6):
            act_cols[comp] = jnp.broadcast_to(wide[0:HALF, comp : comp + 1], (HALF, LANES))

    def forces(step, begin, end, fresh_start):
        def group(g, _):
            rows = pl.ds(pl.multiple_of(g * 8, 8), 8)
            act = [act_cols[comp, rows, :] for comp in range(6)]

            def tile(t, sums):
                parts = [field[step, t, n : n + 1, :] for n in range(7)]
                return pair_terms(act, parts, sums)

            if fresh_start:
                start = tuple(jnp.zeros((8, LANES), F32) for _ in range(6))
            else:
                start = tuple(sums_v[rows, n * LANES : (n + 1) * LANES] for n in range(6))
            done = lax.fori_loop(begin, end, tile, start, unroll=16)
            for n in range(6):
                sums_v[rows, n * LANES : (n + 1) * LANES] = done[n]
            return 0

        lax.fori_loop(0, 8, group, 0)

    def all_sums(step):
        lane = lax.broadcasted_iota(jnp.int32, (8, 6 * LANES), 1)
        row = lax.broadcasted_iota(jnp.int32, (8, 6 * LANES), 0)
        ones = jnp.where(jnp.right_shift(lane, 7) == row, 1.0, 0.0).astype(BF16)
        one, two, three = split3(sums_v[...])
        rows = (dot_nt(ones, three) + dot_nt(ones, two)) + dot_nt(ones, one)
        sum_src[step] = jnp.concatenate([rows, jnp.zeros((8, HALF), F32)], axis=1)
        return [
            send(sum_src.at[step], sum_dst.at[step, y], sum_s.at[step, dy], sum_r.at[step, y],
                 device(0, dy, 0, 0))
            for dy in y_list
        ]

    def total_sums(step, copies):
        sum_dst[step, y] = sum_src[step]
        for dy in y_list:
            other = lax.rem(y + dy, ys)
            pltpu.make_async_remote_copy(
                src_ref=sum_src.at[step], dst_ref=sum_dst.at[step, other],
                send_sem=sum_s.at[step, dy], recv_sem=sum_r.at[step, other],
                device_id=device(0, dy, 0, 0), device_id_type=MESH,
            ).wait_recv()
        tile = sum_dst[step, 0]
        for n in range(1, ys):
            tile = tile + sum_dst[step, n]
        return tile

    def correct(act, force):
        other = swap(act)
        pred_pos, pred_vel, mass = act[0:3], act[3:6], act[7:8]
        elapsed = jnp.where(low_lanes()[0:1], act[6:7], 1.0)
        old_acc, old_jerk = other[0:3], other[3:6]
        new_acc, new_jerk = force[0:3], force[3:6]
        sq = elapsed * elapsed
        diff = old_acc - new_acc
        snap = (-6.0 * diff - elapsed * (4.0 * old_jerk + 2.0 * new_jerk)) / sq
        crackle = (12.0 * diff + 6.0 * elapsed * (old_jerk + new_jerk)) / (sq * elapsed)
        pos = pred_pos + sq * sq / 24.0 * snap + sq * sq * elapsed / 120.0 * crackle
        vel = pred_vel + sq * elapsed / 6.0 * snap + sq * sq / 24.0 * crackle
        one = jnp.ones((1, LANES), F32)
        low = jnp.concatenate([pos, vel, one, mass], axis=0)
        high = jnp.concatenate([new_acc, new_jerk, one, one], axis=0)
        return pack(low, high)

    def gather_fresh(step, tile):
        gath[step, 0, 0, 0] = tile
        copies = {}
        for dz, dx in xz_list:
            copies[dz, dx] = send(
                gath.at[step, 0, 0, 0], gath.at[step, 0, dz, dx], ag_s.at[step, dz, dx],
                ag_r.at[step, dz, dx], device(dz, 0, 0, dx),
            )
        return copies

    def finish_gather(step, copies):
        across = []
        for dz in [0] + z_list:
            for dx in range(xs):
                if (dz, dx) != (0, 0):
                    copies[dz, dx].wait_recv()
            across.append(
                send(gath.at[step, 0, dz], gath.at[step, 1, dz], agc_s.at[step, dz],
                     agc_r.at[step, dz], device(0, 0, 1, 0))
            )
        for copy in across:
            copy.wait_recv()
        for px in range(xs):
            for pz in range(zs):
                dz, dx = lax.rem(z - pz + zs, zs), lax.rem(x - px + xs, xs)
                tile0 = gath[step, c, dz, dx]
                tile1 = gath[step, 1 - c, dz, dx]
                at = (px * zs + pz) * LANES
                corr[step, 0:8, at : at + LANES] = jnp.where(low_lanes(), tile0, swap(tile1))
                corr[step, 8:16, at : at + LANES] = jnp.where(low_lanes(), swap(tile0), tile1)

    chunks = total // LANES
    names = [0, 1, 2, 3, 4, 5, 8, 9, 10, 11, 12, 13]

    def build_low_hot(step):
        def one(n, _):
            at = pl.multiple_of(n * LANES, LANES)
            low_hot[step, :, pl.ds(at, LANES)] = low_hot_of(step, at)
            return 0

        lax.fori_loop(0, chunks, one, 0)

    def hits(step):
        def one(n, _):
            at = pl.multiple_of(n * LANES, LANES)
            hot = jnp.where(high_hot(step, at), 1.0, 0.0)
            left[0:16, pl.ds(at, LANES)] = jnp.concatenate([hot, hot], axis=0).astype(BF16)
            return 0

        lax.fori_loop(0, chunks, one, 0, unroll=2)
        return dot_nt(left[0:16, :], low_hot[step])[0:8]

    def build_match():
        at = pl.multiple_of(x * quarter + z * LANES, LANES)
        mine = act_v[1:2, pl.ds(at, LANES)].astype(F32)
        column[...] = jnp.broadcast_to(mine, (LANES, LANES)).T
        own = column[pl.ds(pl.multiple_of(c * HALF, HALF), HALF), :]

        def one(n, _):
            at = pl.multiple_of(n * LANES, LANES)
            row = act_v[0:1, pl.ds(at, LANES)].astype(F32)
            match[:, pl.ds(at, LANES)] = jnp.where(own == row, 1.0, 0.0).astype(BF16)
            return 0

        lax.fori_loop(0, chunks, one, 0)

    def place(step, hit):
        def one(n, _):
            at = pl.multiple_of(n * LANES, LANES)
            mine = high_hot(step, at)
            pieces = split3(corr[step, :, pl.ds(at, LANES)])
            for p, piece in enumerate(pieces):
                wide = piece.astype(F32)
                rows = [jnp.where(mine, wide[v : v + 1], 0.0) for v in names]
                left[p * 96 : p * 96 + 96, pl.ds(at, LANES)] = jnp.concatenate(rows, axis=0).astype(BF16)
            return 0

        lax.fori_loop(0, chunks, one, 0, unroll=2)
        got = dot_nt(left[...], low_hot[step])
        scat[...] = (got[192:288] + got[96:192]) + got[0:96]
        taken = hit > 0.5
        for n, v in enumerate(names):
            at = v * 8
            raw[at : at + 8, :] = jnp.where(taken, scat[n * 8 : n * 8 + 8, :], raw[at : at + 8, :])
        raw[48:56, :] = jnp.where(taken, STEP * (step + 1), raw[48:56, :])

    def write_state(step):
        for n, v in enumerate(names):
            state_out[n, step : step + 1, :] = corr[step, v : v + 1, :]

    pick(0, src0)
    pl.semaphore_wait(barrier, len(partners))
    rs0 = scatter_picks(0)
    f0, across0 = send_field(0)
    pick(1, raw)
    build_low_hot(0)
    ar0 = reduce_picks(0, rs0)
    hit0 = hits(0)
    fresh[0] = hit0
    rows1, _ = predicted(2 * STEP)
    lay_field(1, rows1, jnp.where(hit0 > 0.5, 0.0, value(raw, 7)))
    pass_on(0, f0, across0)
    act0 = picked(0, ar0)
    rs1 = scatter_picks(1)
    f1, across1 = send_field(1)
    set_columns(act0)
    forces(0, 0, zs * block, True)
    for copy in across0:
        copy.wait_recv()
    forces(0, zs * block, 2 * zs * block, False)
    s0 = all_sums(0)
    ar1 = reduce_picks(1, rs1)
    build_match()
    force0 = total_sums(0, s0)
    fresh0 = gather_fresh(0, correct(act0, force0))
    pass_on(1, f1, across1)
    build_low_hot(1)
    fresh[1] = hits(1)
    act1_raw = picked(1, ar1)
    for copy in across1:
        copy.wait_recv()
    finish_gather(0, fresh0)

    extra = total // ys
    for n in range(extra // LANES):
        at = pl.multiple_of(y * extra + n * LANES, LANES)
        low = corr[0, 0:8, pl.ds(at, LANES)]
        high = corr[0, 8:16, pl.ds(at, LANES)]
        new_pos, new_vel = predict(low[0:3], low[3:6], high[0:3], high[3:6], 2 * STEP - STEP)
        field[1, 2 * zs * block + n] = jnp.concatenate(
            [new_pos, new_vel, low[7:8], jnp.zeros((1, LANES), F32)], axis=0
        )
    found = exact_nt(corr[0], match[...])
    found = jnp.concatenate([found, jnp.zeros((16, HALF), F32)], axis=1)
    again = found[14:15] > 0.5
    low = jnp.where(again, found[0:8], act1_raw)
    high = jnp.where(again, found[8:16], swap(act1_raw))
    last = jnp.where(again, STEP, act1_raw[6:7])
    elapsed1 = 2 * STEP - last
    pos1, vel1 = predict(low[0:3], low[3:6], high[0:3], high[3:6], elapsed1)
    act1 = pack(jnp.concatenate([pos1, vel1, elapsed1, low[7:8]], axis=0), high)
    set_columns(act1)
    forces(1, 0, 2 * zs * block + extra // LANES, True)
    s1 = all_sums(1)
    place(0, fresh[0])
    write_state(0)
    force1 = total_sums(1, s1)
    fresh1 = gather_fresh(1, correct(act1, force1))
    finish_gather(1, fresh1)
    write_state(1)
    place(1, fresh[1])
    for ref, at in ((pos_out, 0), (vel_out, 3), (acc_out, 8), (jerk_out, 11)):
        for comp in range(3):
            for hi in range(8):
                row = (at + comp) * 8 + hi
                ref[comp : comp + 1, hi * LANES : (hi + 1) * LANES] = raw[row : row + 1, :]
    time_out[...] = raw[48:56, :]
    for copy in started:
        copy.wait_send()


def hand_on(*refs):
    srcs, dsts, sem = refs[0:6], refs[6:12], refs[12]
    stores = [pltpu.make_async_copy(a, b, sem.at[n]) for n, (a, b) in enumerate(zip(srcs, dsts))]
    for store in reversed(stores):
        store.start()
    for store in stores:
        store.wait()


def run(sizes, *args):
    zs, ys, xs = sizes
    total = xs * zs * LANES
    vmem = pltpu.VMEM
    dma = pltpu.SemaphoreType.DMA
    tiles = 2 * zs * 8 + total // ys // LANES
    scratch = [
        vmem((3, 1024), F32), vmem((3, 1024), F32), vmem((3, 1024), F32), vmem((3, 1024), F32),
        vmem((8, LANES), F32), vmem((8, LANES), F32), vmem((2, total), jnp.int32),
        vmem((112, LANES), F32), vmem((112, LANES), F32),
        vmem((2, zs, CORES, 8, LANES), F32), vmem((2, zs, CORES, 8, LANES), F32),
        vmem((2, 8, LANES), F32), vmem((2, ys, 8, LANES), F32),
        vmem((2, 8, LANES), F32), vmem((2, ys, 8, LANES), F32),
        vmem((2, tiles, 8, LANES), F32),
        vmem((2, CORES, zs, xs, 8, LANES), F32),
        vmem((6, HALF, LANES), F32), vmem((HALF, 6 * LANES), F32),
        vmem((2, 16, total), F32), vmem((2, LANES, total), BF16), vmem((HALF, total), BF16),
        vmem((LANES, LANES), F32), vmem((96, LANES), F32), vmem((2, 8, LANES), F32),
        vmem((288, total), BF16),
        dma((7,)),
        dma((2, zs, CORES)), dma((2, zs, CORES)),
        dma((2, ys)), dma((2, ys)), dma((2, ys)), dma((2, ys)),
        dma((2, zs)), dma((2, zs)), dma((2, zs)), dma((2, zs)),
        dma((2, zs, xs)), dma((2, zs, xs)), dma((2, zs)), dma((2, zs)),
    ]
    flat = jax.ShapeDtypeStruct((3, 1024), F32)
    out_shape = [flat, flat, flat, flat, jax.ShapeDtypeStruct((8, LANES), F32),
                 jax.ShapeDtypeStruct((12, 2, total), F32)]
    args = [pltpu.with_memory_space_constraint(arg, pltpu.HBM) for arg in args]
    results = pl.pallas_call(
        functools.partial(kernel, sizes),
        out_shape=[pltpu.VMEM(out.shape, F32) for out in out_shape],
        in_specs=[pl.BlockSpec(memory_space=pltpu.HBM)] * 7,
        out_specs=[pl.BlockSpec(memory_space=pltpu.VMEM)] * 6,
        scratch_shapes=scratch,
        compiler_params=pltpu.CompilerParams(
            collective_id=0, has_side_effects=True, vmem_limit_bytes=40 << 20
        ),
        name="hermite",
    )(*args)
    return pl.pallas_call(
        hand_on,
        out_shape=out_shape,
        in_specs=[pl.BlockSpec(memory_space=pltpu.VMEM)] * 6,
        out_specs=[pl.BlockSpec(memory_space=pl.ANY)] * 6,
        scratch_shapes=[dma((6,))],
        compiler_params=pltpu.CompilerParams(vmem_limit_bytes=40 << 20),
        name="finish",
    )(*results)


def per_device(sizes, positions, velocities, accels, jerks, masses, last_time, active):
    pos, vel, acc, jerk, times, state = run(
        sizes, positions, velocities, accels, jerks,
        masses.reshape(8, LANES), last_time.reshape(8, LANES), active,
    )
    return pos, vel, acc, jerk, times.reshape(8 * LANES), state.transpose(1, 0, 2)


def solution(mesh, sizes=(RINGS["z"], RINGS["y"], RINGS["x"])):
    in_specs = (P(None, "ja"), P(None, "ja"), P(None, "ja"), P(None, "ja"), P("ja"), P("ja"), P())
    out_specs = (P(None, "ja"), P(None, "ja"), P(None, "ja"), P(None, "ja"), P("ja"), P())
    return jax.shard_map(
        functools.partial(per_device, sizes), mesh=mesh, in_specs=in_specs, out_specs=out_specs,
        check_vma=False,
    )
```

```python
import functools

import jax
import jax.numpy as jnp
from jax import lax
from jax.experimental import pallas as pl
from jax.experimental.pallas import tpu as pltpu
from jax.sharding import PartitionSpec as P

MESH = pl.DeviceIdType.MESH
F32 = jnp.float32
BF16 = jnp.bfloat16
STEP = 0.0625
SOFT_SQ = 0.0025
LANES = 128
HALF = 64
CORES = 2
DEPTH = 16
RINGS = {"z": 8, "y": 8, "x": 4}


def split3(value):
    first = value.astype(BF16)
    rest = value - first.astype(F32)
    second = rest.astype(BF16)
    third = (rest - second.astype(F32)).astype(BF16)
    return first, second, third


def dot_nn(left, right):
    return lax.dot_general(left, right, (((1,), (0,)), ((), ())), preferred_element_type=F32)


def dot_nt(left, right):
    return lax.dot_general(left, right, (((1,), (1,)), ((), ())), preferred_element_type=F32)


def exact_nn(left, onehot):
    one, two, three = split3(left)
    return (dot_nn(three, onehot) + dot_nn(two, onehot)) + dot_nn(one, onehot)


def exact_nt(left, onehot):
    one, two, three = split3(left)
    return (dot_nt(three, onehot) + dot_nt(two, onehot)) + dot_nt(one, onehot)


def predict(pos, vel, acc, jerk, elapsed):
    pred_pos = pos + elapsed * (vel + elapsed * (acc / 2.0 + elapsed * jerk / 6.0))
    pred_vel = vel + elapsed * (acc + elapsed * jerk / 2.0)
    return pred_pos, pred_vel


def low_lanes():
    return lax.broadcasted_iota(jnp.int32, (8, LANES), 1) < HALF


def swap(tile):
    return pltpu.roll(tile, HALF, 1)


def pack(low, high):
    return jnp.where(low_lanes(), low, swap(high))


def pair_weights(act, field):
    ax, ay, az, au, av, aw = act
    fx, fy, fz, fu, fv, fw = field
    dx, dy, dz = fx - ax, fy - ay, fz - az
    du, dv, dw = fu - au, fv - av, fw - aw
    dist_sq = (dx * dx + dy * dy) + (dz * dz + SOFT_SQ)
    inv = lax.rsqrt(dist_sq)
    inv_sq = inv * inv
    cubed = inv * inv_sq
    return cubed, (((dx * du + dy * dv) + dz * dw) * inv_sq) * cubed


def split2(value):
    first = value.astype(BF16)
    return first, (value - first.astype(F32)).astype(BF16)


def hops(delta, size):
    return min(delta, size - delta)


def kernel(
    sizes,
    pos_in, vel_in, acc_in, jerk_in, mass_in, last_in, act_in,
    pos_out, vel_out, acc_out, jerk_out, time_out, state_out,
    pos_v, vel_v, acc_v, jerk_v, mass_v, last_v, act_v,
    raw, src0, rs_src, rs_dst, pick_src, pick_dst, sum_src, sum_dst,
    field, gath, act_cols, feat, centre, corr, low_hot, match, column, scat, fresh, left, left_c, right_c, ahead, coming,
    in_sem, rs_s, rs_r, pick_s, pick_r, sum_s, sum_r, fz_s, fz_r, fc_s, fc_r,
    ag_s, ag_r, agc_s, agc_r, an_s, an_r, anc_s, anc_r,
):
    zs, ys, xs = sizes
    total = xs * zs * LANES
    quarter = zs * LANES
    ja = lax.axis_index("ja")
    x = lax.axis_index("ia")
    z = lax.div(ja, ys * CORES)
    y = lax.rem(lax.div(ja, CORES), ys)
    c = lax.rem(ja, CORES)

    def device(dz, dy, dc, dx):
        pz = lax.rem(z + dz, zs)
        py = lax.rem(y + dy, ys)
        pc = lax.rem(c + dc, CORES)
        return ((pz * ys + py) * CORES + pc, lax.rem(x + dx, xs))

    zc_list = sorted(
        [(dz, dc) for dz in range(zs) for dc in range(CORES) if (dz, dc) != (0, 0)],
        key=lambda p: -hops(p[0], zs),
    )
    xz_list = sorted(
        [(dz, dx) for dz in range(zs) for dx in range(xs) if (dz, dx) != (0, 0)],
        key=lambda p: -hops(p[0], zs) - hops(p[1], xs),
    )
    y_list = sorted(range(1, ys), key=lambda p: -hops(p, ys))
    z_list = sorted(range(1, zs), key=lambda p: hops(p, zs))
    started = []

    def send(src, dst, ssem, rsem, target):
        copy = pltpu.make_async_remote_copy(
            src_ref=src, dst_ref=dst, send_sem=ssem, recv_sem=rsem,
            device_id=target, device_id_type=MESH,
        )
        copy.start()
        started.append(copy)
        return copy

    loads = [
        pltpu.make_async_copy(a, b, in_sem.at[n])
        for n, (a, b) in enumerate(
            [(pos_in, pos_v), (vel_in, vel_v), (acc_in, acc_v), (jerk_in, jerk_v),
             (mass_in, mass_v), (last_in, last_v), (act_in, act_v)]
        )
    ]
    for load in loads:
        load.start()
    barrier = pltpu.get_barrier_semaphore()
    partners = [(dz, 0, dc, 0) for dz, dc in zc_list]
    partners += [(0, dy, 0, 0) for dy in y_list]
    partners += [(dz, 0, 0, dx) for dz, dx in xz_list if dx != 0]
    for partner in partners:
        pl.semaphore_signal(barrier, inc=1, device_id=device(*partner), device_id_type=MESH)
    for load in loads:
        load.wait()

    for ref, at in ((pos_v, 0), (vel_v, 3), (acc_v, 8), (jerk_v, 11)):
        for comp in range(3):
            for hi in range(8):
                row = (at + comp) * 8 + hi
                raw[row : row + 1, :] = ref[comp : comp + 1, hi * LANES : (hi + 1) * LANES]
    raw[48:56, :] = last_v[...]
    raw[56:64, :] = mass_v[...]

    def value(ref, n):
        return ref[n * 8 : n * 8 + 8, :]

    def predicted(time_now):
        elapsed = time_now - value(raw, 6)
        rows = []
        for comp in range(3):
            rows.append(
                predict(value(raw, comp), value(raw, 3 + comp), value(raw, 8 + comp),
                        value(raw, 11 + comp), elapsed)
            )
        return [r[0] for r in rows] + [r[1] for r in rows], elapsed

    def lay_field(step, rows, mass):
        for n, row in enumerate(rows + [mass]):
            field[step, 0:8, n, :] = row
        field[step, 0:8, 7, :] = jnp.zeros((8, LANES), F32)

    rows0, elapsed0 = predicted(STEP)
    for n, row in enumerate(rows0):
        src0[n * 8 : n * 8 + 8, :] = row
    src0[48:56, :] = elapsed0
    src0[56:112, :] = raw[56:112, :]
    lay_field(0, rows0, value(raw, 7))
    for n, row in enumerate(rows0):
        middle = jnp.sum(jnp.sum(row, axis=0, keepdims=True), axis=1, keepdims=True) / (8.0 * LANES)
        centre[n : n + 1, :] = jnp.broadcast_to(middle, (1, LANES))
    centre[6:8, :] = jnp.zeros((2, LANES), F32)

    sub = lax.broadcasted_iota(jnp.int32, (LANES, LANES), 0)
    sub8 = lax.broadcasted_iota(jnp.int32, (8, LANES), 0)
    first_star = ja * (8 * LANES)

    def high_hot(step, at):
        local = act_v[step : step + 1, pl.ds(at, LANES)] - first_star
        return jnp.right_shift(local, 7) == sub8

    def low_hot_of(step, at):
        lo = jnp.bitwise_and(act_v[step : step + 1, pl.ds(at, LANES)], LANES - 1)
        return jnp.where(lo == sub, 1.0, 0.0).astype(BF16)

    def pick(step, source):
        pieces = split3(source[...])
        for pz in range(zs):
            at = pl.multiple_of(x * quarter + pz * LANES, LANES)
            hot = low_hot_of(step, at)
            got = (dot_nn(pieces[2], hot) + dot_nn(pieces[1], hot)) + dot_nn(pieces[0], hot)
            own = jnp.where(high_hot(step, at)[None], got.reshape(14, 8, LANES), 0.0)
            rows = jnp.concatenate([jnp.sum(own, axis=1), jnp.zeros((2, LANES), F32)], axis=0)
            low, high = rows[0:8], rows[8:16]
            rs_src[step, pz, 0] = jnp.where(low_lanes(), low, swap(high))
            rs_src[step, pz, 1] = jnp.where(low_lanes(), swap(low), high)

    def scatter_picks(step):
        copies = []
        for dz, dc in zc_list:
            pz, pc = lax.rem(z + dz, zs), lax.rem(c + dc, CORES)
            copies.append(
                send(rs_src.at[step, pz, pc], rs_dst.at[step, dz, dc], rs_s.at[step, dz, dc],
                     rs_r.at[step, dz, dc], device(dz, 0, dc, 0))
            )
        return copies

    def reduce_picks(step, copies):
        for copy in copies:
            copy.wait_recv()
        tile = rs_src[step, z, c]
        for dz, dc in zc_list:
            tile = tile + rs_dst[step, dz, dc]
        pick_src[step] = tile
        return [
            send(pick_src.at[step], pick_dst.at[step, dy], pick_s.at[step, dy],
                 pick_r.at[step, dy], device(0, dy, 0, 0))
            for dy in y_list
        ]

    def picked(step, copies):
        for copy in copies:
            copy.wait_recv()
        tile = pick_src[step]
        for dy in y_list:
            tile = tile + pick_dst[step, dy]
        return tile

    block = 8

    def send_field(step):
        copies = []
        for dz in z_list:
            copies.append(
                send(field.at[step, pl.ds(0, block)], field.at[step, pl.ds(dz * block, block)],
                     fz_s.at[step, dz], fz_r.at[step, dz], device(dz, 0, 0, 0))
            )
        across = [forward(step, 0)]
        return copies, across

    def forward(step, dz):
        return send(
            field.at[step, pl.ds(dz * block, block)],
            field.at[step, pl.ds((zs + dz) * block, block)],
            fc_s.at[step, dz], fc_r.at[step, dz], device(0, 0, 1, 0),
        )

    def pass_on(step, copies, across):
        for dz, copy in zip(z_list, copies):
            copy.wait_recv()
            across.append(forward(step, dz))

    def set_columns(tile):
        wide = jnp.concatenate([tile, jnp.zeros((LANES - 8, LANES), F32)], axis=0).T
        for comp in range(6):
            act_cols[comp] = jnp.broadcast_to(wide[0:HALF, comp : comp + 1], (HALF, LANES))

    def build_features(step, begin, end):
        row = lax.broadcasted_iota(jnp.int32, (8, LANES), 0)

        def one(t, _):
            tile = field[step, t]
            mass = tile[6:7]
            own = jnp.where(row < 6, (tile - centre[...]) * mass, jnp.where(row == 6, mass, 0.0))
            pieces = [piece.astype(F32) for piece in split3(own)] + [jnp.zeros((8, LANES), F32)]
            at = pl.multiple_of(t * LANES, LANES)
            feat[:, pl.ds(at, LANES)] = jnp.concatenate(pieces, axis=0).astype(BF16)
            return 0

        lax.fori_loop(begin, end, one, 0, unroll=4 if (end - begin) % 4 == 0 else 2)

    def forces(step, tile, tiles):
        def weights(t):
            parts = {key: [] for key in ("w_hi", "w_lo", "q_hi", "q_lo")}
            for pair in range(4):
                ws, qs = [], []
                for k in range(2):
                    near = [field[step, t * 2 + k, n : n + 1, :] for n in range(6)]
                    both = [
                        pair_weights([act_cols[n, g * 8 : g * 8 + 8, :] for n in range(6)], near)
                        for g in (2 * pair, 2 * pair + 1)
                    ]
                    ws.append(jnp.concatenate([b[0] for b in both], axis=0))
                    qs.append(jnp.concatenate([b[1] for b in both], axis=0))
                for key, cols in (("w", ws), ("q", qs)):
                    high, low = split2(jnp.concatenate(cols, axis=1))
                    parts[key + "_hi"].append(high)
                    parts[key + "_lo"].append(low)
            return (jnp.concatenate(parts["w_hi"] + parts["q_hi"], axis=0),
                    jnp.concatenate(parts["w_lo"] + parts["q_lo"], axis=0))

        def add(sums, t, pieces):
            here = feat[:, pl.ds(pl.multiple_of(t * 2 * LANES, 2 * LANES), 2 * LANES)]
            return tuple(total + dot_nt(here, piece) for total, piece in zip(sums, pieces))

        def run_of(first, count, sums):
            held = None
            for n in range(count):
                now = weights(first + n)
                if held is not None:
                    sums = add(sums, first + n - 1, held)
                held = now
            return add(sums, first + count - 1, held)

        whole, rest = divmod(tiles // 2, DEPTH)
        sums = (jnp.zeros((32, LANES), F32), jnp.zeros((32, LANES), F32))
        if whole:
            sums = lax.fori_loop(0, whole, lambda n, held: run_of(n * DEPTH, DEPTH, held), sums)
        if rest:
            sums = run_of(whole * DEPTH, rest, sums)
        both = sums[0] + sums[1]
        by_w = (both[16:24] + both[8:16]) + both[0:8]
        by_q = swap(by_w)
        off = tile - centre[...]
        acc = by_w[0:3] - off[0:3] * by_w[6:7]
        jerk = (by_w[3:6] - off[3:6] * by_w[6:7]) - 3.0 * (by_q[0:3] - off[0:3] * by_q[6:7])
        low = lax.broadcasted_iota(jnp.int32, (3, LANES), 1) < HALF
        sum_src[step, 0:3] = jnp.where(low, acc, swap(jerk))

    def send_sums(step):
        return [
            send(sum_src.at[step, pl.ds(0, 3)], sum_dst.at[step, y, pl.ds(0, 3)],
                 sum_s.at[step, dy], sum_r.at[step, y],
                 device(0, dy, 0, 0))
            for dy in y_list
        ]

    def total_sums(step, copies):
        sum_dst[step, y, 0:3] = sum_src[step, 0:3]
        for dy in y_list:
            other = lax.rem(y + dy, ys)
            pltpu.make_async_remote_copy(
                src_ref=sum_src.at[step, pl.ds(0, 3)],
                dst_ref=sum_dst.at[step, other, pl.ds(0, 3)],
                send_sem=sum_s.at[step, dy], recv_sem=sum_r.at[step, other],
                device_id=device(0, dy, 0, 0), device_id_type=MESH,
            ).wait_recv()
        tile = sum_dst[step, 0, 0:3]
        for n in range(1, ys):
            tile = tile + sum_dst[step, n, 0:3]
        return tile, swap(tile)

    def correct(act, force):
        other = swap(act)
        pred_pos, pred_vel, mass = act[0:3], act[3:6], act[7:8]
        elapsed = jnp.where(low_lanes()[0:1], act[6:7], 1.0)
        old_acc, old_jerk = other[0:3], other[3:6]
        new_acc, new_jerk = force
        sq = elapsed * elapsed
        diff = old_acc - new_acc
        snap = (-6.0 * diff - elapsed * (4.0 * old_jerk + 2.0 * new_jerk)) / sq
        crackle = (12.0 * diff + 6.0 * elapsed * (old_jerk + new_jerk)) / (sq * elapsed)
        pos = pred_pos + sq * sq / 24.0 * snap + sq * sq * elapsed / 120.0 * crackle
        vel = pred_vel + sq * elapsed / 6.0 * snap + sq * sq / 24.0 * crackle
        return pos, vel, new_acc, new_jerk

    def gather_fresh(step, rows):
        two = jnp.ones((2, LANES), F32)
        gath[step, 0, 0, 0] = pack(
            jnp.concatenate([rows[0], rows[1], two], axis=0),
            jnp.concatenate([rows[2], rows[3], two], axis=0),
        )
        return {
            (dz, dx): send(
                gath.at[step, 0, 0, 0, pl.ds(0, 6)], gath.at[step, 0, dz, dx, pl.ds(0, 6)],
                ag_s.at[step, dz, dx], ag_r.at[step, dz, dx], device(dz, 0, 0, dx),
            )
            for dz, dx in xz_list
        }

    def gather_next(rows, mass):
        pos, vel = predict(*rows, 2 * STEP - STEP)
        all_rows = jnp.concatenate([pos, vel, mass, jnp.ones((1, LANES), F32)], axis=0)
        low = lax.broadcasted_iota(jnp.int32, (4, LANES), 1) < HALF
        ahead[0, 0, 0] = jnp.where(low, all_rows[0:4], swap(all_rows)[4:8])
        return {
            (dz, dx): send(
                ahead.at[0, 0, 0], ahead.at[0, dz, dx],
                an_s.at[dz, dx], an_r.at[dz, dx], device(dz, 0, 0, dx),
            )
            for dz, dx in xz_list
        }

    def by_chunks(copies, forward_chunk, take):
        order = [0] + z_list
        across = []
        for n, dz in enumerate(order):
            for dx in range(xs):
                if (dz, dx) != (0, 0):
                    copies[dz, dx].wait_recv()
            across.append(forward_chunk(dz))
        for copy, dz in zip(across, order):
            copy.wait_recv()
            take(dz)

    def forward_fresh(step):
        return lambda dz: send(
            gath.at[step, 0, dz, :, pl.ds(0, 6)], gath.at[step, 1, dz, :, pl.ds(0, 6)],
            agc_s.at[step, dz], agc_r.at[step, dz], device(0, 0, 1, 0),
        )

    def forward_next(dz):
        return send(ahead.at[0, dz], ahead.at[1, dz], anc_s.at[dz], anc_r.at[dz], device(0, 0, 1, 0))

    def place_of(dz, dx):
        pz, px = lax.rem(z - dz + zs, zs), lax.rem(x - dx + xs, xs)
        return pl.multiple_of((px * zs + pz) * LANES, LANES)

    def take_next(dz):
        low = lax.broadcasted_iota(jnp.int32, (4, LANES), 1) < HALF
        for dx in range(xs):
            at = place_of(dz, dx)
            tile0, tile1 = ahead[c, dz, dx], ahead[1 - c, dz, dx]
            coming[0:4, pl.ds(at, LANES)] = jnp.where(low, tile0, swap(tile1))
            coming[4:8, pl.ds(at, LANES)] = jnp.where(low, swap(tile0), tile1)

    def both_cores(step, dz, dx):
        tile0, tile1 = gath[step, c, dz, dx], gath[step, 1 - c, dz, dx]
        return (jnp.where(low_lanes(), tile0, swap(tile1)),
                jnp.where(low_lanes(), swap(tile0), tile1))

    def take_fresh(dz):
        for dx in range(xs):
            at = place_of(dz, dx)
            low, high = both_cores(0, dz, dx)
            corr[0:8, pl.ds(at, LANES)] = low
            corr[8:16, pl.ds(at, LANES)] = high

    def masked_pieces(step, at, low, high):
        mine = high_hot(step, at)
        rows = []
        for piece in split3(jnp.concatenate([low, high], axis=0)):
            wide = piece.astype(F32)
            rows += [jnp.where(mine, wide[v : v + 1], 0.0) for v in names]
        return jnp.concatenate(rows, axis=0).astype(BF16)

    def take_last(dz):
        for dx in range(xs):
            at = place_of(dz, dx)
            low, high = both_cores(1, dz, dx)
            for n in range(6):
                state_out[n, 1:2, pl.ds(at, LANES)] = low[n : n + 1]
                state_out[6 + n, 1:2, pl.ds(at, LANES)] = high[n : n + 1]
            here = slice(dx * LANES, (dx + 1) * LANES)
            left_c[:, here] = masked_pieces(1, at, low, high)
            right_c[:, here] = low_hot[1, :, pl.ds(at, LANES)]
        scat[...] += dot_nt(left_c[...], right_c[...])

    chunks = total // LANES
    names = [0, 1, 2, 3, 4, 5, 8, 9, 10, 11, 12, 13]

    def build_low_hot(step):
        def one(n, _):
            at = pl.multiple_of(n * LANES, LANES)
            low_hot[step, :, pl.ds(at, LANES)] = low_hot_of(step, at)
            return 0

        lax.fori_loop(0, chunks, one, 0)

    def hits(step):
        def one(n, _):
            at = pl.multiple_of(n * LANES, LANES)
            hot = jnp.where(high_hot(step, at), 1.0, 0.0)
            left[0:16, pl.ds(at, LANES)] = jnp.concatenate([hot, hot], axis=0).astype(BF16)
            return 0

        lax.fori_loop(0, chunks, one, 0, unroll=2)
        return dot_nt(left[0:16, :], low_hot[step])[0:8]

    def build_match():
        at = pl.multiple_of(x * quarter + z * LANES, LANES)
        mine = act_v[1:2, pl.ds(at, LANES)].astype(F32)
        column[...] = jnp.broadcast_to(mine, (LANES, LANES)).T
        own = column[pl.ds(pl.multiple_of(c * HALF, HALF), HALF), :]

        def one(n, _):
            at = pl.multiple_of(n * LANES, LANES)
            row = act_v[0:1, pl.ds(at, LANES)].astype(F32)
            match[:, pl.ds(at, LANES)] = jnp.where(own == row, 1.0, 0.0).astype(BF16)
            return 0

        lax.fori_loop(0, chunks, one, 0)

    def settle(step):
        taken = fresh[step] > 0.5
        for n, v in enumerate(names):
            at, row = v * 8, n * 8
            new = (scat[192 + row : 200 + row, :] + scat[96 + row : 104 + row, :]) + scat[row : row + 8, :]
            raw[at : at + 8, :] = jnp.where(taken, new, raw[at : at + 8, :])
        raw[48:56, :] = jnp.where(taken, STEP * (step + 1), raw[48:56, :])

    def place_first():
        def one(n, _):
            at = pl.multiple_of(n * LANES, LANES)
            tiles = corr[:, pl.ds(at, LANES)]
            left[:, pl.ds(at, LANES)] = masked_pieces(0, at, tiles[0:8], tiles[8:16])
            return 0

        lax.fori_loop(0, chunks, one, 0, unroll=2)
        scat[...] = dot_nt(left[...], low_hot[0])
        settle(0)
        for n, v in enumerate(names):
            state_out[n, 0:1, :] = corr[v : v + 1, :]

    pick(0, src0)
    pl.semaphore_wait(barrier, len(partners))
    rs0 = scatter_picks(0)
    f0, across0 = send_field(0)
    pick(1, raw)
    build_low_hot(0)
    ar0 = reduce_picks(0, rs0)
    hit0 = hits(0)
    fresh[0] = hit0
    rows1, _ = predicted(2 * STEP)
    lay_field(1, rows1, jnp.where(hit0 > 0.5, 0.0, value(raw, 7)))
    pass_on(0, f0, across0)
    build_features(0, 0, zs * block)
    act0 = picked(0, ar0)
    rs1 = scatter_picks(1)
    f1, across1 = send_field(1)
    set_columns(act0)
    for copy in across0:
        copy.wait_recv()
    build_features(0, zs * block, 2 * zs * block)
    forces(0, act0, 2 * zs * block)
    s0 = send_sums(0)
    ar1 = reduce_picks(1, rs1)
    build_match()
    force0 = total_sums(0, s0)
    rows_a = correct(act0, force0)
    next0 = gather_next(rows_a, act0[7:8])
    fresh0 = gather_fresh(0, rows_a)
    pass_on(1, f1, across1)
    build_low_hot(1)
    fresh[1] = hits(1)
    act1_raw = picked(1, ar1)
    raw_high = swap(act1_raw)
    raw_elapsed = 2 * STEP - act1_raw[6:7]
    raw_pos, raw_vel = predict(
        act1_raw[0:3], act1_raw[3:6], raw_high[0:3], raw_high[3:6], raw_elapsed
    )
    for copy in across1:
        copy.wait_recv()
    build_features(1, 0, 2 * zs * block)
    by_chunks(next0, forward_next, take_next)

    extra = total // ys
    for n in range(extra // LANES):
        at = pl.multiple_of(y * extra + n * LANES, LANES)
        field[1, 2 * zs * block + n] = coming[:, pl.ds(at, LANES)]
    found = exact_nt(coming[...], match[...])
    found = jnp.concatenate([found, jnp.zeros((8, HALF), F32)], axis=1)
    again = found[7:8] > 0.5
    elapsed1 = jnp.where(again, 2 * STEP - STEP, raw_elapsed)
    ahead1 = jnp.where(again, found[0:6], jnp.concatenate([raw_pos, raw_vel], axis=0))
    low1 = jnp.concatenate([ahead1, elapsed1, act1_raw[7:8]], axis=0)
    set_columns(low1)
    build_features(1, 2 * zs * block, 2 * zs * block + extra // LANES)
    forces(1, low1, 2 * zs * block + extra // LANES)
    s1 = send_sums(1)
    by_chunks(fresh0, forward_fresh(0), take_fresh)
    held = jnp.concatenate([exact_nt(corr[8:16, :], match[...]), jnp.zeros((8, HALF), F32)], axis=1)
    act1 = pack(low1, jnp.where(again, held, raw_high))
    force1 = total_sums(1, s1)
    fresh1 = gather_fresh(1, correct(act1, force1))
    place_first()
    scat[...] = jnp.zeros((288, LANES), F32)
    by_chunks(fresh1, forward_fresh(1), take_last)
    settle(1)
    for ref, at in ((pos_out, 0), (vel_out, 3), (acc_out, 8), (jerk_out, 11)):
        for comp in range(3):
            for hi in range(8):
                row = (at + comp) * 8 + hi
                ref[comp : comp + 1, hi * LANES : (hi + 1) * LANES] = raw[row : row + 1, :]
    time_out[...] = raw[48:56, :]
    for copy in started:
        copy.wait_send()


def hand_on(*refs):
    srcs, dsts, sem = refs[0:6], refs[6:12], refs[12]
    stores = [pltpu.make_async_copy(a, b, sem.at[n]) for n, (a, b) in enumerate(zip(srcs, dsts))]
    for store in reversed(stores):
        store.start()
    for store in stores:
        store.wait()


def run(sizes, *args):
    zs, ys, xs = sizes
    total = xs * zs * LANES
    vmem = pltpu.VMEM
    dma = pltpu.SemaphoreType.DMA
    tiles = 2 * zs * 8 + total // ys // LANES
    scratch = [
        vmem((3, 1024), F32), vmem((3, 1024), F32), vmem((3, 1024), F32), vmem((3, 1024), F32),
        vmem((8, LANES), F32), vmem((8, LANES), F32), vmem((2, total), jnp.int32),
        vmem((112, LANES), F32), vmem((112, LANES), F32),
        vmem((2, zs, CORES, 8, LANES), F32), vmem((2, zs, CORES, 8, LANES), F32),
        vmem((2, 8, LANES), F32), vmem((2, ys, 8, LANES), F32),
        vmem((2, 8, LANES), F32), vmem((2, ys, 8, LANES), F32),
        vmem((2, tiles, 8, LANES), F32),
        vmem((2, CORES, zs, xs, 8, LANES), F32),
        vmem((6, HALF, LANES), F32), vmem((32, tiles * LANES), BF16), vmem((8, LANES), F32),
        vmem((16, total), F32), vmem((2, LANES, total), BF16), vmem((HALF, total), BF16),
        vmem((LANES, LANES), F32), vmem((288, LANES), F32), vmem((2, 8, LANES), F32),
        vmem((288, total), BF16), vmem((288, xs * LANES), BF16), vmem((LANES, xs * LANES), BF16),
        vmem((CORES, zs, xs, 4, LANES), F32), vmem((8, total), F32),
        dma((7,)),
        dma((2, zs, CORES)), dma((2, zs, CORES)),
        dma((2, ys)), dma((2, ys)), dma((2, ys)), dma((2, ys)),
        dma((2, zs)), dma((2, zs)), dma((2, zs)), dma((2, zs)),
        dma((2, zs, xs)), dma((2, zs, xs)), dma((2, zs)), dma((2, zs)),
        dma((zs, xs)), dma((zs, xs)), dma((zs,)), dma((zs,)),
    ]
    flat = jax.ShapeDtypeStruct((3, 1024), F32)
    out_shape = [flat, flat, flat, flat, jax.ShapeDtypeStruct((8, LANES), F32),
                 jax.ShapeDtypeStruct((12, 2, total), F32)]
    args = [pltpu.with_memory_space_constraint(arg, pltpu.HBM) for arg in args]
    results = pl.pallas_call(
        functools.partial(kernel, sizes),
        out_shape=[pltpu.VMEM(out.shape, F32) for out in out_shape],
        in_specs=[pl.BlockSpec(memory_space=pltpu.HBM)] * 7,
        out_specs=[pl.BlockSpec(memory_space=pltpu.VMEM)] * 6,
        scratch_shapes=scratch,
        compiler_params=pltpu.CompilerParams(
            collective_id=0, has_side_effects=True, vmem_limit_bytes=40 << 20
        ),
        name="hermite",
    )(*args)
    return pl.pallas_call(
        hand_on,
        out_shape=out_shape,
        in_specs=[pl.BlockSpec(memory_space=pltpu.VMEM)] * 6,
        out_specs=[pl.BlockSpec(memory_space=pl.ANY)] * 6,
        scratch_shapes=[dma((6,))],
        compiler_params=pltpu.CompilerParams(vmem_limit_bytes=40 << 20),
        name="finish",
    )(*results)


def per_device(sizes, positions, velocities, accels, jerks, masses, last_time, active):
    pos, vel, acc, jerk, times, state = run(
        sizes, positions, velocities, accels, jerks,
        masses.reshape(8, LANES), last_time.reshape(8, LANES), active,
    )
    return pos, vel, acc, jerk, times.reshape(8 * LANES), state.transpose(1, 0, 2)


def solution(mesh, sizes=(RINGS["z"], RINGS["y"], RINGS["x"])):
    in_specs = (P(None, "ja"), P(None, "ja"), P(None, "ja"), P(None, "ja"), P("ja"), P("ja"), P())
    out_specs = (P(None, "ja"), P(None, "ja"), P(None, "ja"), P(None, "ja"), P("ja"), P())
    return jax.shard_map(
        functools.partial(per_device, sizes), mesh=mesh, in_specs=in_specs, out_specs=out_specs,
        check_vma=False,
    )
```

```python
import functools

import jax
import jax.numpy as jnp
from jax import lax
from jax.experimental import pallas as pl
from jax.experimental.pallas import tpu as pltpu
from jax.sharding import PartitionSpec as P

MESH = pl.DeviceIdType.MESH
F32 = jnp.float32
BF16 = jnp.bfloat16
STEP = 0.0625
SOFT_SQ = 0.0025
LANES = 128
HALF = 64
CORES = 2
DEPTH = 32
RINGS = {"z": 8, "y": 8, "x": 4}


def split3(value):
    first = value.astype(BF16)
    rest = value - first.astype(F32)
    second = rest.astype(BF16)
    third = (rest - second.astype(F32)).astype(BF16)
    return first, second, third


def dot_nn(left, right):
    return lax.dot_general(left, right, (((1,), (0,)), ((), ())), preferred_element_type=F32)


def dot_nt(left, right):
    return lax.dot_general(left, right, (((1,), (1,)), ((), ())), preferred_element_type=F32)


def exact_nn(left, onehot):
    one, two, three = split3(left)
    return (dot_nn(three, onehot) + dot_nn(two, onehot)) + dot_nn(one, onehot)


def exact_nt(left, onehot):
    one, two, three = split3(left)
    return (dot_nt(three, onehot) + dot_nt(two, onehot)) + dot_nt(one, onehot)


def predict(pos, vel, acc, jerk, elapsed):
    pred_pos = pos + elapsed * (vel + elapsed * (acc / 2.0 + elapsed * jerk / 6.0))
    pred_vel = vel + elapsed * (acc + elapsed * jerk / 2.0)
    return pred_pos, pred_vel


def low_lanes():
    return lax.broadcasted_iota(jnp.int32, (8, LANES), 1) < HALF


def swap(tile):
    return pltpu.roll(tile, HALF, 1)


def pack(low, high):
    return jnp.where(low_lanes(), low, swap(high))


def pair_weights(act, field):
    ax, ay, az, au, av, aw = act
    fx, fy, fz, fu, fv, fw = field
    dx, dy, dz = fx - ax, fy - ay, fz - az
    du, dv, dw = fu - au, fv - av, fw - aw
    dist_sq = (dx * dx + dy * dy) + (dz * dz + SOFT_SQ)
    inv = lax.rsqrt(dist_sq)
    inv_sq = inv * inv
    cubed = inv * inv_sq
    return cubed, (((dx * du + dy * dv) + dz * dw) * inv_sq) * cubed


def split2(value):
    first = value.astype(BF16)
    return first, (value - first.astype(F32)).astype(BF16)


def hops(delta, size):
    return min(delta, size - delta)


def kernel(
    sizes,
    pos_in, vel_in, acc_in, jerk_in, mass_in, last_in, act_in,
    pos_out, vel_out, acc_out, jerk_out, time_out, state_out,
    pos_v, vel_v, acc_v, jerk_v, mass_v, last_v, act_v,
    raw, src0, rs_src, rs_dst, pick_src, pick_dst, sum_src, sum_dst,
    field, gath, act_cols, feat, centre, corr, low_hot, match, column, scat, fresh, left, left_c, right_c, ahead, coming,
    in_sem, rs_s, rs_r, pick_s, pick_r, sum_s, sum_r, fz_s, fz_r, fc_s, fc_r,
    met, ag_s, ag_r, agc_s, agc_r, an_s, an_r, anc_s, anc_r,
):
    zs, ys, xs = sizes
    total = xs * zs * LANES
    quarter = zs * LANES
    ja = lax.axis_index("ja")
    x = lax.axis_index("ia")
    z = lax.div(ja, ys * CORES)
    y = lax.rem(lax.div(ja, CORES), ys)
    c = lax.rem(ja, CORES)

    def device(dz, dy, dc, dx):
        pz = lax.rem(z + dz, zs)
        py = lax.rem(y + dy, ys)
        pc = lax.rem(c + dc, CORES)
        return ((pz * ys + py) * CORES + pc, lax.rem(x + dx, xs))

    zc_list = sorted(
        [(dz, dc) for dz in range(zs) for dc in range(CORES) if (dz, dc) != (0, 0)],
        key=lambda p: -hops(p[0], zs),
    )
    xz_list = sorted(
        [(dz, dx) for dz in range(zs) for dx in range(xs) if (dz, dx) != (0, 0)],
        key=lambda p: -hops(p[0], zs) - hops(p[1], xs),
    )
    y_list = sorted(range(1, ys), key=lambda p: -hops(p, ys))
    z_list = sorted(range(1, zs), key=lambda p: hops(p, zs))
    started = []
    drained = []

    def drain(count):
        for copy in started[len(drained) : count]:
            copy.wait_send()
            drained.append(copy)

    def send(src, dst, ssem, rsem, target):
        copy = pltpu.make_async_remote_copy(
            src_ref=src, dst_ref=dst, send_sem=ssem, recv_sem=rsem,
            device_id=target, device_id_type=MESH,
        )
        copy.start()
        started.append(copy)
        return copy

    loads = [
        pltpu.make_async_copy(a, b, in_sem.at[n])
        for n, (a, b) in enumerate(
            [(pos_in, pos_v), (vel_in, vel_v), (acc_in, acc_v), (jerk_in, jerk_v),
             (mass_in, mass_v), (last_in, last_v), (act_in, act_v)]
        )
    ]
    for load in loads:
        load.start()
    barrier = pltpu.get_barrier_semaphore()
    partners = [(dz, 0, dc, 0) for dz, dc in zc_list]
    partners += [(0, dy, 0, 0) for dy in y_list]
    partners += [(0, 0, 0, dx) for dx in range(1, xs)]
    for partner in partners:
        pl.semaphore_signal(barrier, inc=1, device_id=device(*partner), device_id_type=MESH)
    for load in loads:
        load.wait()

    for ref, at in ((pos_v, 0), (vel_v, 3), (acc_v, 8), (jerk_v, 11)):
        for comp in range(3):
            for hi in range(8):
                row = (at + comp) * 8 + hi
                raw[row : row + 1, :] = ref[comp : comp + 1, hi * LANES : (hi + 1) * LANES]
    raw[48:56, :] = last_v[...]
    raw[56:64, :] = mass_v[...]

    def value(ref, n):
        return ref[n * 8 : n * 8 + 8, :]

    def predicted(time_now):
        elapsed = time_now - value(raw, 6)
        rows = []
        for comp in range(3):
            rows.append(
                predict(value(raw, comp), value(raw, 3 + comp), value(raw, 8 + comp),
                        value(raw, 11 + comp), elapsed)
            )
        return [r[0] for r in rows] + [r[1] for r in rows], elapsed

    def lay_field(step, rows, mass):
        for n, row in enumerate(rows + [mass]):
            field[step, 0:8, n, :] = row
        field[step, 0:8, 7, :] = jnp.zeros((8, LANES), F32)

    rows0, elapsed0 = predicted(STEP)
    for n, row in enumerate(rows0):
        src0[n * 8 : n * 8 + 8, :] = row
    src0[48:56, :] = elapsed0
    src0[56:112, :] = raw[56:112, :]

    sub = lax.broadcasted_iota(jnp.int32, (LANES, LANES), 0)
    sub8 = lax.broadcasted_iota(jnp.int32, (8, LANES), 0)
    first_star = ja * (8 * LANES)

    def high_hot(step, at):
        local = act_v[step : step + 1, pl.ds(at, LANES)] - first_star
        return jnp.right_shift(local, 7) == sub8

    def low_hot_of(step, at):
        lo = jnp.bitwise_and(act_v[step : step + 1, pl.ds(at, LANES)], LANES - 1)
        return jnp.where(lo == sub, 1.0, 0.0).astype(BF16)

    def pick(step, source):
        pieces = split3(source[...])
        for pz in range(zs):
            at = pl.multiple_of(x * quarter + pz * LANES, LANES)
            hot = low_hot_of(step, at)
            got = (dot_nn(pieces[2], hot) + dot_nn(pieces[1], hot)) + dot_nn(pieces[0], hot)
            own = jnp.where(high_hot(step, at)[None], got.reshape(14, 8, LANES), 0.0)
            rows = jnp.concatenate([jnp.sum(own, axis=1), jnp.zeros((2, LANES), F32)], axis=0)
            low, high = rows[0:8], rows[8:16]
            rs_src[step, pz, 0] = jnp.where(low_lanes(), low, swap(high))
            rs_src[step, pz, 1] = jnp.where(low_lanes(), swap(low), high)

    def scatter_picks(step):
        copies = []
        for dz, dc in zc_list:
            pz, pc = lax.rem(z + dz, zs), lax.rem(c + dc, CORES)
            copies.append(
                send(rs_src.at[step, pz, pc], rs_dst.at[step, dz, dc], rs_s.at[step, dz, dc],
                     rs_r.at[step, dz, dc], device(dz, 0, dc, 0))
            )
        return copies

    def reduce_picks(step, copies):
        for copy in copies:
            copy.wait_recv()
        tile = rs_src[step, z, c]
        for dz, dc in zc_list:
            tile = tile + rs_dst[step, dz, dc]
        pick_src[step] = tile
        return [
            send(pick_src.at[step], pick_dst.at[step, dy], pick_s.at[step, dy],
                 pick_r.at[step, dy], device(0, dy, 0, 0))
            for dy in y_list
        ]

    def picked(step, copies):
        for copy in copies:
            copy.wait_recv()
        tile = pick_src[step]
        for dy in y_list:
            tile = tile + pick_dst[step, dy]
        return tile

    block = 8

    def send_field(step):
        copies = []
        for dz in z_list:
            copies.append(
                send(field.at[step, pl.ds(0, block)], field.at[step, pl.ds(dz * block, block)],
                     fz_s.at[step, dz], fz_r.at[step, dz], device(dz, 0, 0, 0))
            )
        across = [forward(step, 0)]
        return copies, across

    def forward(step, dz):
        return send(
            field.at[step, pl.ds(dz * block, block)],
            field.at[step, pl.ds((zs + dz) * block, block)],
            fc_s.at[step, dz], fc_r.at[step, dz], device(0, 0, 1, 0),
        )

    def pass_on(step, copies, across):
        for dz, copy in zip(z_list, copies):
            copy.wait_recv()
            across.append(forward(step, dz))

    def set_columns(tile):
        wide = jnp.concatenate([tile, jnp.zeros((LANES - 8, LANES), F32)], axis=0).T
        for comp in range(6):
            act_cols[comp] = jnp.broadcast_to(wide[0:HALF, comp : comp + 1], (HALF, LANES))

    def build_features(step, begin, end):
        row = lax.broadcasted_iota(jnp.int32, (8, LANES), 0)

        def one(t, _):
            tile = field[step, t]
            mass = tile[6:7]
            own = jnp.where(row < 6, (tile - centre[...]) * mass, jnp.where(row == 6, mass, 0.0))
            pieces = [piece.astype(F32) for piece in split3(own)] + [jnp.zeros((8, LANES), F32)]
            at = pl.multiple_of(t * LANES, LANES)
            feat[:, pl.ds(at, LANES)] = jnp.concatenate(pieces, axis=0).astype(BF16)
            return 0

        lax.fori_loop(begin, end, one, 0, unroll=4 if (end - begin) % 4 == 0 else 2)

    def forces(step, tile, tiles):
        def weights(t):
            parts = {key: [] for key in ("w_hi", "w_lo", "q_hi", "q_lo")}
            for pair in range(4):
                ws, qs = [], []
                for k in range(2):
                    near = [field[step, t * 2 + k, n : n + 1, :] for n in range(6)]
                    both = [
                        pair_weights([act_cols[n, g * 8 : g * 8 + 8, :] for n in range(6)], near)
                        for g in (2 * pair, 2 * pair + 1)
                    ]
                    ws.append(jnp.concatenate([b[0] for b in both], axis=0))
                    qs.append(jnp.concatenate([b[1] for b in both], axis=0))
                for key, cols in (("w", ws), ("q", qs)):
                    high, low = split2(jnp.concatenate(cols, axis=1))
                    parts[key + "_hi"].append(high)
                    parts[key + "_lo"].append(low)
            return (jnp.concatenate(parts["w_hi"] + parts["q_hi"], axis=0),
                    jnp.concatenate(parts["w_lo"] + parts["q_lo"], axis=0))

        def add(sums, t, pieces):
            here = feat[:, pl.ds(pl.multiple_of(t * 2 * LANES, 2 * LANES), 2 * LANES)]
            return tuple(total + dot_nt(here, piece) for total, piece in zip(sums, pieces))

        def run_of(first, count, sums):
            held = None
            for n in range(count):
                now = weights(first + n)
                if held is not None:
                    sums = add(sums, first + n - 1, held)
                held = now
            return add(sums, first + count - 1, held)

        whole, rest = divmod(tiles // 2, DEPTH)
        sums = (jnp.zeros((32, LANES), F32), jnp.zeros((32, LANES), F32))
        if whole:
            sums = lax.fori_loop(0, whole, lambda n, held: run_of(n * DEPTH, DEPTH, held), sums)
        if rest:
            sums = run_of(whole * DEPTH, rest, sums)
        both = sums[0] + sums[1]
        by_w = (both[16:24] + both[8:16]) + both[0:8]
        by_q = swap(by_w)
        off = tile - centre[...]
        acc = by_w[0:3] - off[0:3] * by_w[6:7]
        jerk = (by_w[3:6] - off[3:6] * by_w[6:7]) - 3.0 * (by_q[0:3] - off[0:3] * by_q[6:7])
        low = lax.broadcasted_iota(jnp.int32, (3, LANES), 1) < HALF
        sum_src[step, 0:3] = jnp.where(low, acc, swap(jerk))

    def send_sums(step):
        return [
            send(sum_src.at[step, pl.ds(0, 3)], sum_dst.at[step, y, pl.ds(0, 3)],
                 sum_s.at[step, dy], sum_r.at[step, y],
                 device(0, dy, 0, 0))
            for dy in y_list
        ]

    def total_sums(step, copies):
        sum_dst[step, y, 0:3] = sum_src[step, 0:3]
        for dy in y_list:
            other = lax.rem(y + dy, ys)
            pltpu.make_async_remote_copy(
                src_ref=sum_src.at[step, pl.ds(0, 3)],
                dst_ref=sum_dst.at[step, other, pl.ds(0, 3)],
                send_sem=sum_s.at[step, dy], recv_sem=sum_r.at[step, other],
                device_id=device(0, dy, 0, 0), device_id_type=MESH,
            ).wait_recv()
        tile = sum_dst[step, 0, 0:3]
        for n in range(1, ys):
            tile = tile + sum_dst[step, n, 0:3]
        return tile, swap(tile)

    def correct(act, force):
        other = swap(act)
        pred_pos, pred_vel, mass = act[0:3], act[3:6], act[7:8]
        elapsed = jnp.where(low_lanes()[0:1], act[6:7], 1.0)
        old_acc, old_jerk = other[0:3], other[3:6]
        new_acc, new_jerk = force
        sq = elapsed * elapsed
        diff = old_acc - new_acc
        snap = (-6.0 * diff - elapsed * (4.0 * old_jerk + 2.0 * new_jerk)) / sq
        crackle = (12.0 * diff + 6.0 * elapsed * (old_jerk + new_jerk)) / (sq * elapsed)
        pos = pred_pos + sq * sq / 24.0 * snap + sq * sq * elapsed / 120.0 * crackle
        vel = pred_vel + sq * elapsed / 6.0 * snap + sq * sq / 24.0 * crackle
        return pos, vel, new_acc, new_jerk

    def gather_fresh(step, rows):
        two = jnp.ones((2, LANES), F32)
        gath[step, 0, 0, 0] = pack(
            jnp.concatenate([rows[0], rows[1], two], axis=0),
            jnp.concatenate([rows[2], rows[3], two], axis=0),
        )
        return {
            (dz, dx): send(
                gath.at[step, 0, 0, 0, pl.ds(0, 6)], gath.at[step, 0, dz, dx, pl.ds(0, 6)],
                ag_s.at[step, dz, dx], ag_r.at[step, dz, dx], device(dz, 0, 0, dx),
            )
            for dz, dx in xz_list
        }

    def gather_next(rows, mass):
        pos, vel = predict(*rows, 2 * STEP - STEP)
        all_rows = jnp.concatenate([pos, vel, mass, jnp.ones((1, LANES), F32)], axis=0)
        low = lax.broadcasted_iota(jnp.int32, (4, LANES), 1) < HALF
        ahead[0, 0, 0] = jnp.where(low, all_rows[0:4], swap(all_rows)[4:8])
        return {
            (dz, dx): send(
                ahead.at[0, 0, 0], ahead.at[0, dz, dx],
                an_s.at[dz, dx], an_r.at[dz, dx], device(dz, 0, 0, dx),
            )
            for dz, dx in xz_list
        }

    def by_chunks(copies, forward_chunk, take):
        order = [0] + z_list
        across = []
        for n, dz in enumerate(order):
            for dx in range(xs):
                if (dz, dx) != (0, 0):
                    copies[dz, dx].wait_recv()
            across.append(forward_chunk(dz))
        for copy, dz in zip(across, order):
            copy.wait_recv()
            take(dz)

    def forward_fresh(step):
        return lambda dz: send(
            gath.at[step, 0, dz, :, pl.ds(0, 6)], gath.at[step, 1, dz, :, pl.ds(0, 6)],
            agc_s.at[step, dz], agc_r.at[step, dz], device(0, 0, 1, 0),
        )

    def forward_next(dz):
        return send(ahead.at[0, dz], ahead.at[1, dz], anc_s.at[dz], anc_r.at[dz], device(0, 0, 1, 0))

    def place_of(dz, dx):
        pz, px = lax.rem(z - dz + zs, zs), lax.rem(x - dx + xs, xs)
        return pl.multiple_of((px * zs + pz) * LANES, LANES)

    def take_next(dz):
        low = lax.broadcasted_iota(jnp.int32, (4, LANES), 1) < HALF
        for dx in range(xs):
            at = place_of(dz, dx)
            tile0, tile1 = ahead[c, dz, dx], ahead[1 - c, dz, dx]
            coming[0:4, pl.ds(at, LANES)] = jnp.where(low, tile0, swap(tile1))
            coming[4:8, pl.ds(at, LANES)] = jnp.where(low, swap(tile0), tile1)

    def both_cores(step, dz, dx):
        tile0, tile1 = gath[step, c, dz, dx], gath[step, 1 - c, dz, dx]
        return (jnp.where(low_lanes(), tile0, swap(tile1)),
                jnp.where(low_lanes(), swap(tile0), tile1))

    def take_fresh(dz):
        for dx in range(xs):
            at = place_of(dz, dx)
            low, high = both_cores(0, dz, dx)
            corr[0:8, pl.ds(at, LANES)] = low
            corr[8:16, pl.ds(at, LANES)] = high

    def masked_pieces(step, at, low, high):
        mine = high_hot(step, at)
        rows = []
        for piece in split3(jnp.concatenate([low, high], axis=0)):
            wide = piece.astype(F32)
            rows += [jnp.where(mine, wide[v : v + 1], 0.0) for v in names]
        return jnp.concatenate(rows, axis=0).astype(BF16)

    def take_last(dz):
        for dx in range(xs):
            at = place_of(dz, dx)
            low, high = both_cores(1, dz, dx)
            for n in range(6):
                state_out[n, 1:2, pl.ds(at, LANES)] = low[n : n + 1]
                state_out[6 + n, 1:2, pl.ds(at, LANES)] = high[n : n + 1]
            here = slice(dx * LANES, (dx + 1) * LANES)
            left_c[:, here] = masked_pieces(1, at, low, high)
            right_c[:, here] = low_hot[1, :, pl.ds(at, LANES)]
        scat[...] += dot_nt(left_c[...], right_c[...])

    chunks = total // LANES
    names = [0, 1, 2, 3, 4, 5, 8, 9, 10, 11, 12, 13]

    def build_low_hot(step):
        def one(n, _):
            at = pl.multiple_of(n * LANES, LANES)
            low_hot[step, :, pl.ds(at, LANES)] = low_hot_of(step, at)
            return 0

        lax.fori_loop(0, chunks, one, 0)

    def hits(step):
        def one(n, _):
            at = pl.multiple_of(n * LANES, LANES)
            hot = jnp.where(high_hot(step, at), 1.0, 0.0)
            left[0:16, pl.ds(at, LANES)] = jnp.concatenate([hot, hot], axis=0).astype(BF16)
            return 0

        lax.fori_loop(0, chunks, one, 0, unroll=2)
        return dot_nt(left[0:16, :], low_hot[step])[0:8]

    def build_match():
        at = pl.multiple_of(x * quarter + z * LANES, LANES)
        mine = act_v[1:2, pl.ds(at, LANES)].astype(F32)
        column[...] = jnp.broadcast_to(mine, (LANES, LANES)).T
        own = column[pl.ds(pl.multiple_of(c * HALF, HALF), HALF), :]

        def one(n, _):
            at = pl.multiple_of(n * LANES, LANES)
            row = act_v[0:1, pl.ds(at, LANES)].astype(F32)
            match[:, pl.ds(at, LANES)] = jnp.where(own == row, 1.0, 0.0).astype(BF16)
            return 0

        lax.fori_loop(0, chunks, one, 0)

    def settle(step):
        taken = fresh[step] > 0.5
        for n, v in enumerate(names):
            at, row = v * 8, n * 8
            new = (scat[192 + row : 200 + row, :] + scat[96 + row : 104 + row, :]) + scat[row : row + 8, :]
            raw[at : at + 8, :] = jnp.where(taken, new, raw[at : at + 8, :])
        raw[48:56, :] = jnp.where(taken, STEP * (step + 1), raw[48:56, :])

    def place_first():
        def one(n, _):
            at = pl.multiple_of(n * LANES, LANES)
            tiles = corr[:, pl.ds(at, LANES)]
            left[:, pl.ds(at, LANES)] = masked_pieces(0, at, tiles[0:8], tiles[8:16])
            return 0

        lax.fori_loop(0, chunks, one, 0, unroll=2)
        scat[...] = dot_nt(left[...], low_hot[0])
        settle(0)
        for n, v in enumerate(names):
            state_out[n, 0:1, :] = corr[v : v + 1, :]

    pick(0, src0)
    pl.semaphore_wait(barrier, len(partners))
    rs0 = scatter_picks(0)
    lay_field(0, rows0, value(raw, 7))
    f0, across0 = send_field(0)
    for n, row in enumerate(rows0):
        middle = jnp.sum(jnp.sum(row, axis=0, keepdims=True), axis=1, keepdims=True) / (8.0 * LANES)
        centre[n : n + 1, :] = jnp.broadcast_to(middle, (1, LANES))
    centre[6:8, :] = jnp.zeros((2, LANES), F32)
    pick(1, raw)
    build_low_hot(0)
    ar0 = reduce_picks(0, rs0)
    for dx in range(1, xs):
        pl.semaphore_signal(met, inc=1, device_id=device(0, 0, 0, dx), device_id_type=MESH)
    hit0 = hits(0)
    fresh[0] = hit0
    rows1, _ = predicted(2 * STEP)
    lay_field(1, rows1, jnp.where(hit0 > 0.5, 0.0, value(raw, 7)))
    pass_on(0, f0, across0)
    build_features(0, 0, zs * block)
    act0 = picked(0, ar0)
    rs1 = scatter_picks(1)
    f1, across1 = send_field(1)
    set_columns(act0)
    for copy in across0:
        copy.wait_recv()
    build_features(0, zs * block, 2 * zs * block)
    forces(0, act0, 2 * zs * block)
    early = len(started)
    s0 = send_sums(0)
    ar1 = reduce_picks(1, rs1)
    build_match()
    force0 = total_sums(0, s0)
    rows_a = correct(act0, force0)
    pl.semaphore_wait(met, xs - 1)
    next0 = gather_next(rows_a, act0[7:8])
    fresh0 = gather_fresh(0, rows_a)
    pass_on(1, f1, across1)
    build_low_hot(1)
    fresh[1] = hits(1)
    drain(early)
    act1_raw = picked(1, ar1)
    raw_high = swap(act1_raw)
    raw_elapsed = 2 * STEP - act1_raw[6:7]
    raw_pos, raw_vel = predict(
        act1_raw[0:3], act1_raw[3:6], raw_high[0:3], raw_high[3:6], raw_elapsed
    )
    for copy in across1:
        copy.wait_recv()
    build_features(1, 0, 2 * zs * block)
    by_chunks(next0, forward_next, take_next)

    extra = total // ys
    for n in range(extra // LANES):
        at = pl.multiple_of(y * extra + n * LANES, LANES)
        field[1, 2 * zs * block + n] = coming[:, pl.ds(at, LANES)]
    found = exact_nt(coming[...], match[...])
    found = jnp.concatenate([found, jnp.zeros((8, HALF), F32)], axis=1)
    again = found[7:8] > 0.5
    elapsed1 = jnp.where(again, 2 * STEP - STEP, raw_elapsed)
    ahead1 = jnp.where(again, found[0:6], jnp.concatenate([raw_pos, raw_vel], axis=0))
    low1 = jnp.concatenate([ahead1, elapsed1, act1_raw[7:8]], axis=0)
    set_columns(low1)
    build_features(1, 2 * zs * block, 2 * zs * block + extra // LANES)
    forces(1, low1, 2 * zs * block + extra // LANES)
    s1 = send_sums(1)
    by_chunks(fresh0, forward_fresh(0), take_fresh)
    held = jnp.concatenate([exact_nt(corr[8:16, :], match[...]), jnp.zeros((8, HALF), F32)], axis=1)
    act1 = pack(low1, jnp.where(again, held, raw_high))
    force1 = total_sums(1, s1)
    late = len(started)
    fresh1 = gather_fresh(1, correct(act1, force1))
    place_first()
    drain(late)
    scat[...] = jnp.zeros((288, LANES), F32)
    by_chunks(fresh1, forward_fresh(1), take_last)
    settle(1)
    for ref, at in ((pos_out, 0), (vel_out, 3), (acc_out, 8), (jerk_out, 11)):
        for comp in range(3):
            for hi in range(8):
                row = (at + comp) * 8 + hi
                ref[comp : comp + 1, hi * LANES : (hi + 1) * LANES] = raw[row : row + 1, :]
    time_out[...] = raw[48:56, :]
    drain(len(started))


def hand_on(*refs):
    srcs, dsts, sem = refs[0:6], refs[6:12], refs[12]
    stores = [pltpu.make_async_copy(a, b, sem.at[n]) for n, (a, b) in enumerate(zip(srcs, dsts))]
    for store in reversed(stores):
        store.start()
    for store in stores:
        store.wait()


def run(sizes, *args):
    zs, ys, xs = sizes
    total = xs * zs * LANES
    vmem = pltpu.VMEM
    dma = pltpu.SemaphoreType.DMA
    tiles = 2 * zs * 8 + total // ys // LANES
    scratch = [
        vmem((3, 1024), F32), vmem((3, 1024), F32), vmem((3, 1024), F32), vmem((3, 1024), F32),
        vmem((8, LANES), F32), vmem((8, LANES), F32), vmem((2, total), jnp.int32),
        vmem((112, LANES), F32), vmem((112, LANES), F32),
        vmem((2, zs, CORES, 8, LANES), F32), vmem((2, zs, CORES, 8, LANES), F32),
        vmem((2, 8, LANES), F32), vmem((2, ys, 8, LANES), F32),
        vmem((2, 8, LANES), F32), vmem((2, ys, 8, LANES), F32),
        vmem((2, tiles, 8, LANES), F32),
        vmem((2, CORES, zs, xs, 8, LANES), F32),
        vmem((6, HALF, LANES), F32), vmem((32, tiles * LANES), BF16), vmem((8, LANES), F32),
        vmem((16, total), F32), vmem((2, LANES, total), BF16), vmem((HALF, total), BF16),
        vmem((LANES, LANES), F32), vmem((288, LANES), F32), vmem((2, 8, LANES), F32),
        vmem((288, total), BF16), vmem((288, xs * LANES), BF16), vmem((LANES, xs * LANES), BF16),
        vmem((CORES, zs, xs, 4, LANES), F32), vmem((8, total), F32),
        dma((7,)),
        dma((2, zs, CORES)), dma((2, zs, CORES)),
        dma((2, ys)), dma((2, ys)), dma((2, ys)), dma((2, ys)),
        dma((2, zs)), dma((2, zs)), dma((2, zs)), dma((2, zs)),
        pltpu.SemaphoreType.REGULAR,
        dma((2, zs, xs)), dma((2, zs, xs)), dma((2, zs)), dma((2, zs)),
        dma((zs, xs)), dma((zs, xs)), dma((zs,)), dma((zs,)),
    ]
    flat = jax.ShapeDtypeStruct((3, 1024), F32)
    out_shape = [flat, flat, flat, flat, jax.ShapeDtypeStruct((8, LANES), F32),
                 jax.ShapeDtypeStruct((12, 2, total), F32)]
    args = [pltpu.with_memory_space_constraint(arg, pltpu.HBM) for arg in args]
    results = pl.pallas_call(
        functools.partial(kernel, sizes),
        out_shape=[pltpu.VMEM(out.shape, F32) for out in out_shape],
        in_specs=[pl.BlockSpec(memory_space=pltpu.HBM)] * 7,
        out_specs=[pl.BlockSpec(memory_space=pltpu.VMEM)] * 6,
        scratch_shapes=scratch,
        compiler_params=pltpu.CompilerParams(
            collective_id=0, has_side_effects=True, vmem_limit_bytes=40 << 20
        ),
        name="hermite",
    )(*args)
    return pl.pallas_call(
        hand_on,
        out_shape=out_shape,
        in_specs=[pl.BlockSpec(memory_space=pltpu.VMEM)] * 6,
        out_specs=[pl.BlockSpec(memory_space=pl.ANY)] * 6,
        scratch_shapes=[dma((6,))],
        compiler_params=pltpu.CompilerParams(vmem_limit_bytes=40 << 20),
        name="finish",
    )(*results)


def per_device(sizes, positions, velocities, accels, jerks, masses, last_time, active):
    pos, vel, acc, jerk, times, state = run(
        sizes, positions, velocities, accels, jerks,
        masses.reshape(8, LANES), last_time.reshape(8, LANES), active,
    )
    return pos, vel, acc, jerk, times.reshape(8 * LANES), state.transpose(1, 0, 2)


def solution(mesh, sizes=(RINGS["z"], RINGS["y"], RINGS["x"])):
    in_specs = (P(None, "ja"), P(None, "ja"), P(None, "ja"), P(None, "ja"), P("ja"), P("ja"), P())
    out_specs = (P(None, "ja"), P(None, "ja"), P(None, "ja"), P(None, "ja"), P("ja"), P())
    return jax.shard_map(
        functools.partial(per_device, sizes), mesh=mesh, in_specs=in_specs, out_specs=out_specs,
        check_vma=False,
    )
```

```python
import functools

import jax
import jax.numpy as jnp
from jax import lax
from jax.experimental import pallas as pl
from jax.experimental.pallas import tpu as pltpu
from jax.sharding import PartitionSpec as P

MESH = pl.DeviceIdType.MESH
F32 = jnp.float32
BF16 = jnp.bfloat16
STEP = 0.0625
SOFT_SQ = 0.0025
LANES = 128
HALF = 64
CORES = 2
DEPTH = 32
RINGS = {"z": 8, "y": 8, "x": 4}


def split3(value):
    first = value.astype(BF16)
    rest = value - first.astype(F32)
    second = rest.astype(BF16)
    third = (rest - second.astype(F32)).astype(BF16)
    return first, second, third


def dot_nn(left, right):
    return lax.dot_general(left, right, (((1,), (0,)), ((), ())), preferred_element_type=F32)


def dot_nt(left, right):
    return lax.dot_general(left, right, (((1,), (1,)), ((), ())), preferred_element_type=F32)


def exact_nn(left, onehot):
    one, two, three = split3(left)
    return (dot_nn(three, onehot) + dot_nn(two, onehot)) + dot_nn(one, onehot)


def exact_nt(left, onehot):
    one, two, three = split3(left)
    return (dot_nt(three, onehot) + dot_nt(two, onehot)) + dot_nt(one, onehot)


def predict(pos, vel, acc, jerk, elapsed):
    pred_pos = pos + elapsed * (vel + elapsed * (acc / 2.0 + elapsed * jerk / 6.0))
    pred_vel = vel + elapsed * (acc + elapsed * jerk / 2.0)
    return pred_pos, pred_vel


def low_lanes():
    return lax.broadcasted_iota(jnp.int32, (8, LANES), 1) < HALF


def swap(tile):
    return pltpu.roll(tile, HALF, 1)


def pack(low, high):
    return jnp.where(low_lanes(), low, swap(high))


def pair_weights(act, field):
    ax, ay, az, au, av, aw = act
    fx, fy, fz, fu, fv, fw = field
    dx, dy, dz = fx - ax, fy - ay, fz - az
    du, dv, dw = fu - au, fv - av, fw - aw
    dist_sq = (dx * dx + dy * dy) + (dz * dz + SOFT_SQ)
    inv = lax.rsqrt(dist_sq)
    inv_sq = inv * inv
    cubed = inv * inv_sq
    return cubed, (((dx * du + dy * dv) + dz * dw) * inv_sq) * cubed


def split2(value):
    first = value.astype(BF16)
    return first, (value - first.astype(F32)).astype(BF16)


def hops(delta, size):
    return min(delta, size - delta)


def kernel(
    sizes,
    pos_in, vel_in, acc_in, jerk_in, mass_in, last_in, act_in,
    pos_out, vel_out, acc_out, jerk_out, time_out, state_out,
    pos_v, vel_v, acc_v, jerk_v, mass_v, last_v, act_v,
    raw, src0, rs_src, rs_dst, pick_src, pick_dst, sum_src, sum_dst,
    field, gath, act_cols, feat, centre, corr, low_hot, match, column, scat, fresh, left, ahead, coming,
    in_sem, rs_s, rs_r, pick_s, pick_r, sum_s, sum_r, fz_s, fz_r, fc_s, fc_r,
    met, ag_s, ag_r, agc_s, agc_r, an_s, an_r, anc_s, anc_r,
):
    zs, ys, xs = sizes
    total = xs * zs * LANES
    quarter = zs * LANES
    ja = lax.axis_index("ja")
    x = lax.axis_index("ia")
    z = lax.div(ja, ys * CORES)
    y = lax.rem(lax.div(ja, CORES), ys)
    c = lax.rem(ja, CORES)

    def device(dz, dy, dc, dx):
        pz = lax.rem(z + dz, zs)
        py = lax.rem(y + dy, ys)
        pc = lax.rem(c + dc, CORES)
        return ((pz * ys + py) * CORES + pc, lax.rem(x + dx, xs))

    zc_list = sorted(
        [(dz, dc) for dz in range(zs) for dc in range(CORES) if (dz, dc) != (0, 0)],
        key=lambda p: -hops(p[0], zs),
    )
    xz_list = sorted(
        [(dz, dx) for dz in range(zs) for dx in range(xs) if (dz, dx) != (0, 0)],
        key=lambda p: -hops(p[0], zs) - hops(p[1], xs),
    )
    y_list = sorted(range(1, ys), key=lambda p: -hops(p, ys))
    z_list = sorted(range(1, zs), key=lambda p: hops(p, zs))
    started = []
    drained = []

    def drain(count):
        for copy in started[len(drained) : count]:
            copy.wait_send()
            drained.append(copy)

    def send(src, dst, ssem, rsem, target):
        copy = pltpu.make_async_remote_copy(
            src_ref=src, dst_ref=dst, send_sem=ssem, recv_sem=rsem,
            device_id=target, device_id_type=MESH,
        )
        copy.start()
        started.append(copy)
        return copy

    loads = [
        pltpu.make_async_copy(a, b, in_sem.at[n])
        for n, (a, b) in enumerate(
            [(pos_in, pos_v), (vel_in, vel_v), (acc_in, acc_v), (jerk_in, jerk_v),
             (mass_in, mass_v), (last_in, last_v), (act_in, act_v)]
        )
    ]
    for load in loads:
        load.start()
    barrier = pltpu.get_barrier_semaphore()
    partners = [(dz, 0, dc, 0) for dz, dc in zc_list]
    partners += [(0, dy, 0, 0) for dy in y_list]
    partners += [(0, 0, 0, dx) for dx in range(1, xs)]
    for partner in partners:
        pl.semaphore_signal(barrier, inc=1, device_id=device(*partner), device_id_type=MESH)
    for load in loads:
        load.wait()

    for ref, at in ((pos_v, 0), (vel_v, 3), (acc_v, 8), (jerk_v, 11)):
        for comp in range(3):
            for hi in range(8):
                row = (at + comp) * 8 + hi
                raw[row : row + 1, :] = ref[comp : comp + 1, hi * LANES : (hi + 1) * LANES]
    raw[48:56, :] = last_v[...]
    raw[56:64, :] = mass_v[...]

    def value(ref, n):
        return ref[n * 8 : n * 8 + 8, :]

    def predicted(time_now):
        elapsed = time_now - value(raw, 6)
        rows = []
        for comp in range(3):
            rows.append(
                predict(value(raw, comp), value(raw, 3 + comp), value(raw, 8 + comp),
                        value(raw, 11 + comp), elapsed)
            )
        return [r[0] for r in rows] + [r[1] for r in rows], elapsed

    def lay_field(step, rows, mass):
        for n, row in enumerate(rows + [mass]):
            field[step, 0:8, n, :] = row
        field[step, 0:8, 7, :] = jnp.zeros((8, LANES), F32)

    rows0, elapsed0 = predicted(STEP)
    for n, row in enumerate(rows0):
        src0[n * 8 : n * 8 + 8, :] = row
    src0[48:56, :] = elapsed0
    src0[56:112, :] = raw[56:112, :]

    sub = lax.broadcasted_iota(jnp.int32, (LANES, LANES), 0)
    sub8 = lax.broadcasted_iota(jnp.int32, (8, LANES), 0)
    first_star = ja * (8 * LANES)

    def high_hot(step, at):
        local = act_v[step : step + 1, pl.ds(at, LANES)] - first_star
        return jnp.right_shift(local, 7) == sub8

    def low_hot_of(step, at):
        lo = jnp.bitwise_and(act_v[step : step + 1, pl.ds(at, LANES)], LANES - 1)
        return jnp.where(lo == sub, 1.0, 0.0).astype(BF16)

    def pick(step, source):
        pieces = split3(source[...])
        for pz in range(zs):
            at = pl.multiple_of(x * quarter + pz * LANES, LANES)
            hot = low_hot_of(step, at)
            got = (dot_nn(pieces[2], hot) + dot_nn(pieces[1], hot)) + dot_nn(pieces[0], hot)
            own = jnp.where(high_hot(step, at)[None], got.reshape(14, 8, LANES), 0.0)
            rows = jnp.concatenate([jnp.sum(own, axis=1), jnp.zeros((2, LANES), F32)], axis=0)
            low, high = rows[0:8], rows[8:16]
            rs_src[step, pz, 0] = jnp.where(low_lanes(), low, swap(high))
            rs_src[step, pz, 1] = jnp.where(low_lanes(), swap(low), high)

    def scatter_picks(step):
        copies = []
        for dz, dc in zc_list:
            pz, pc = lax.rem(z + dz, zs), lax.rem(c + dc, CORES)
            copies.append(
                send(rs_src.at[step, pz, pc], rs_dst.at[step, dz, dc], rs_s.at[step, dz, dc],
                     rs_r.at[step, dz, dc], device(dz, 0, dc, 0))
            )
        return copies

    def reduce_picks(step, copies):
        for copy in copies:
            copy.wait_recv()
        tile = rs_src[step, z, c]
        for dz, dc in zc_list:
            tile = tile + rs_dst[step, dz, dc]
        pick_src[step] = tile
        return [
            send(pick_src.at[step], pick_dst.at[step, dy], pick_s.at[step, dy],
                 pick_r.at[step, dy], device(0, dy, 0, 0))
            for dy in y_list
        ]

    def picked(step, copies):
        for copy in copies:
            copy.wait_recv()
        tile = pick_src[step]
        for dy in y_list:
            tile = tile + pick_dst[step, dy]
        return tile

    block = 8

    def send_field(step):
        copies = []
        for dz in z_list:
            copies.append(
                send(field.at[step, pl.ds(0, block)], field.at[step, pl.ds(dz * block, block)],
                     fz_s.at[step, dz], fz_r.at[step, dz], device(dz, 0, 0, 0))
            )
        across = [forward(step, 0)]
        return copies, across

    def forward(step, dz):
        return send(
            field.at[step, pl.ds(dz * block, block)],
            field.at[step, pl.ds((zs + dz) * block, block)],
            fc_s.at[step, dz], fc_r.at[step, dz], device(0, 0, 1, 0),
        )

    def pass_on(step, copies, across):
        for dz, copy in zip(z_list, copies):
            copy.wait_recv()
            across.append(forward(step, dz))

    def set_columns(tile):
        wide = jnp.concatenate([tile, jnp.zeros((LANES - 8, LANES), F32)], axis=0).T
        for comp in range(6):
            act_cols[comp] = jnp.broadcast_to(wide[0:HALF, comp : comp + 1], (HALF, LANES))

    def build_features(step, begin, end):
        row = lax.broadcasted_iota(jnp.int32, (8, LANES), 0)

        def one(t, _):
            tile = field[step, t]
            mass = tile[6:7]
            own = jnp.where(row < 6, (tile - centre[...]) * mass, jnp.where(row == 6, mass, 0.0))
            pieces = [piece.astype(F32) for piece in split3(own)] + [jnp.zeros((8, LANES), F32)]
            at = pl.multiple_of(t * LANES, LANES)
            feat[:, pl.ds(at, LANES)] = jnp.concatenate(pieces, axis=0).astype(BF16)
            return 0

        lax.fori_loop(begin, end, one, 0, unroll=4 if (end - begin) % 4 == 0 else 2)

    def forces(step, tile, tiles):
        def weights(t):
            parts = {key: [] for key in ("w_hi", "w_lo", "q_hi", "q_lo")}
            for pair in range(4):
                ws, qs = [], []
                for k in range(2):
                    near = [field[step, t * 2 + k, n : n + 1, :] for n in range(6)]
                    both = [
                        pair_weights([act_cols[n, g * 8 : g * 8 + 8, :] for n in range(6)], near)
                        for g in (2 * pair, 2 * pair + 1)
                    ]
                    ws.append(jnp.concatenate([b[0] for b in both], axis=0))
                    qs.append(jnp.concatenate([b[1] for b in both], axis=0))
                for key, cols in (("w", ws), ("q", qs)):
                    high, low = split2(jnp.concatenate(cols, axis=1))
                    parts[key + "_hi"].append(high)
                    parts[key + "_lo"].append(low)
            return (jnp.concatenate(parts["w_hi"] + parts["q_hi"], axis=0),
                    jnp.concatenate(parts["w_lo"] + parts["q_lo"], axis=0))

        def add(sums, t, pieces):
            here = feat[:, pl.ds(pl.multiple_of(t * 2 * LANES, 2 * LANES), 2 * LANES)]
            return tuple(total + dot_nt(here, piece) for total, piece in zip(sums, pieces))

        def run_of(first, count, sums):
            held = None
            for n in range(count):
                now = weights(first + n)
                if held is not None:
                    sums = add(sums, first + n - 1, held)
                held = now
            return add(sums, first + count - 1, held)

        whole, rest = divmod(tiles // 2, DEPTH)
        sums = (jnp.zeros((32, LANES), F32), jnp.zeros((32, LANES), F32))
        if whole:
            sums = lax.fori_loop(0, whole, lambda n, held: run_of(n * DEPTH, DEPTH, held), sums)
        if rest:
            sums = run_of(whole * DEPTH, rest, sums)
        both = sums[0] + sums[1]
        by_w = (both[16:24] + both[8:16]) + both[0:8]
        by_q = swap(by_w)
        off = tile - centre[...]
        acc = by_w[0:3] - off[0:3] * by_w[6:7]
        jerk = (by_w[3:6] - off[3:6] * by_w[6:7]) - 3.0 * (by_q[0:3] - off[0:3] * by_q[6:7])
        low = lax.broadcasted_iota(jnp.int32, (3, LANES), 1) < HALF
        sum_src[step, 0:3] = jnp.where(low, acc, swap(jerk))

    def send_sums(step):
        return [
            send(sum_src.at[step, pl.ds(0, 3)], sum_dst.at[step, y, pl.ds(0, 3)],
                 sum_s.at[step, dy], sum_r.at[step, y],
                 device(0, dy, 0, 0))
            for dy in y_list
        ]

    def total_sums(step, copies):
        sum_dst[step, y, 0:3] = sum_src[step, 0:3]
        for dy in y_list:
            other = lax.rem(y + dy, ys)
            pltpu.make_async_remote_copy(
                src_ref=sum_src.at[step, pl.ds(0, 3)],
                dst_ref=sum_dst.at[step, other, pl.ds(0, 3)],
                send_sem=sum_s.at[step, dy], recv_sem=sum_r.at[step, other],
                device_id=device(0, dy, 0, 0), device_id_type=MESH,
            ).wait_recv()
        tile = sum_dst[step, 0, 0:3]
        for n in range(1, ys):
            tile = tile + sum_dst[step, n, 0:3]
        return tile, swap(tile)

    def correct(act, force):
        other = swap(act)
        pred_pos, pred_vel, mass = act[0:3], act[3:6], act[7:8]
        elapsed = jnp.where(low_lanes()[0:1], act[6:7], 1.0)
        old_acc, old_jerk = other[0:3], other[3:6]
        new_acc, new_jerk = force
        sq = elapsed * elapsed
        diff = old_acc - new_acc
        snap = (-6.0 * diff - elapsed * (4.0 * old_jerk + 2.0 * new_jerk)) / sq
        crackle = (12.0 * diff + 6.0 * elapsed * (old_jerk + new_jerk)) / (sq * elapsed)
        pos = pred_pos + sq * sq / 24.0 * snap + sq * sq * elapsed / 120.0 * crackle
        vel = pred_vel + sq * elapsed / 6.0 * snap + sq * sq / 24.0 * crackle
        return pos, vel, new_acc, new_jerk

    def gather_fresh(step, rows):
        two = jnp.ones((2, LANES), F32)
        gath[step, 0, 0, 0] = pack(
            jnp.concatenate([rows[0], rows[1], two], axis=0),
            jnp.concatenate([rows[2], rows[3], two], axis=0),
        )
        return {
            (dz, dx): send(
                gath.at[step, 0, 0, 0, pl.ds(0, 6)], gath.at[step, 0, dz, dx, pl.ds(0, 6)],
                ag_s.at[step, dz, dx], ag_r.at[step, dz, dx], device(dz, 0, 0, dx),
            )
            for dz, dx in xz_list
        }

    def gather_next(rows, mass):
        pos, vel = predict(*rows, 2 * STEP - STEP)
        all_rows = jnp.concatenate([pos, vel, mass, jnp.ones((1, LANES), F32)], axis=0)
        low = lax.broadcasted_iota(jnp.int32, (4, LANES), 1) < HALF
        ahead[0, 0, 0] = jnp.where(low, all_rows[0:4], swap(all_rows)[4:8])
        return {
            (dz, dx): send(
                ahead.at[0, 0, 0], ahead.at[0, dz, dx],
                an_s.at[dz, dx], an_r.at[dz, dx], device(dz, 0, 0, dx),
            )
            for dz, dx in xz_list
        }

    def by_chunks(copies, forward_chunk, take):
        order = [0] + z_list
        across = []
        for n, dz in enumerate(order):
            for dx in range(xs):
                if (dz, dx) != (0, 0):
                    copies[dz, dx].wait_recv()
            across.append(forward_chunk(dz))
        for copy, dz in zip(across, order):
            copy.wait_recv()
            take(dz)

    def forward_fresh(step):
        return lambda dz: send(
            gath.at[step, 0, dz, :, pl.ds(0, 6)], gath.at[step, 1, dz, :, pl.ds(0, 6)],
            agc_s.at[step, dz], agc_r.at[step, dz], device(0, 0, 1, 0),
        )

    def forward_next(dz):
        return send(ahead.at[0, dz], ahead.at[1, dz], anc_s.at[dz], anc_r.at[dz], device(0, 0, 1, 0))

    def place_of(dz, dx):
        pz, px = lax.rem(z - dz + zs, zs), lax.rem(x - dx + xs, xs)
        return pl.multiple_of((px * zs + pz) * LANES, LANES)

    def take_next(dz):
        low = lax.broadcasted_iota(jnp.int32, (4, LANES), 1) < HALF
        for dx in range(xs):
            at = place_of(dz, dx)
            tile0, tile1 = ahead[c, dz, dx], ahead[1 - c, dz, dx]
            coming[0:4, pl.ds(at, LANES)] = jnp.where(low, tile0, swap(tile1))
            coming[4:8, pl.ds(at, LANES)] = jnp.where(low, swap(tile0), tile1)

    def both_cores(step, dz, dx):
        tile0, tile1 = gath[step, c, dz, dx], gath[step, 1 - c, dz, dx]
        return (jnp.where(low_lanes(), tile0, swap(tile1)),
                jnp.where(low_lanes(), swap(tile0), tile1))

    def take_fresh(dz):
        for dx in range(xs):
            at = place_of(dz, dx)
            low, high = both_cores(0, dz, dx)
            corr[0:8, pl.ds(at, LANES)] = low
            corr[8:16, pl.ds(at, LANES)] = high

    def masked_pieces(step, at, low, high):
        mine = high_hot(step, at)
        rows = []
        for piece in split3(jnp.concatenate([low, high], axis=0)):
            wide = piece.astype(F32)
            rows += [jnp.where(mine, wide[v : v + 1], 0.0) for v in names]
        return jnp.concatenate(rows, axis=0).astype(BF16)

    def take_last(dz):
        for dx in range(xs):
            at = place_of(dz, dx)
            low, high = both_cores(1, dz, dx)
            for n in range(6):
                state_out[n, 1:2, pl.ds(at, LANES)] = low[n : n + 1]
                state_out[6 + n, 1:2, pl.ds(at, LANES)] = high[n : n + 1]
            left[:, pl.ds(at, LANES)] = masked_pieces(1, at, low, high)

    chunks = total // LANES
    names = [0, 1, 2, 3, 4, 5, 8, 9, 10, 11, 12, 13]

    def build_low_hot(step):
        def one(n, _):
            at = pl.multiple_of(n * LANES, LANES)
            low_hot[step, :, pl.ds(at, LANES)] = low_hot_of(step, at)
            return 0

        lax.fori_loop(0, chunks, one, 0)

    def hits(step):
        def one(n, _):
            at = pl.multiple_of(n * LANES, LANES)
            hot = jnp.where(high_hot(step, at), 1.0, 0.0)
            left[0:16, pl.ds(at, LANES)] = jnp.concatenate([hot, hot], axis=0).astype(BF16)
            return 0

        lax.fori_loop(0, chunks, one, 0, unroll=2)
        return dot_nt(left[0:16, :], low_hot[step])[0:8]

    def build_match():
        at = pl.multiple_of(x * quarter + z * LANES, LANES)
        mine = act_v[1:2, pl.ds(at, LANES)].astype(F32)
        column[...] = jnp.broadcast_to(mine, (LANES, LANES)).T
        own = column[pl.ds(pl.multiple_of(c * HALF, HALF), HALF), :]

        def one(n, _):
            at = pl.multiple_of(n * LANES, LANES)
            row = act_v[0:1, pl.ds(at, LANES)].astype(F32)
            match[:, pl.ds(at, LANES)] = jnp.where(own == row, 1.0, 0.0).astype(BF16)
            return 0

        lax.fori_loop(0, chunks, one, 0)

    def settle(step):
        taken = fresh[step] > 0.5
        for n, v in enumerate(names):
            at, row = v * 8, n * 8
            new = (scat[192 + row : 200 + row, :] + scat[96 + row : 104 + row, :]) + scat[row : row + 8, :]
            raw[at : at + 8, :] = jnp.where(taken, new, raw[at : at + 8, :])
        raw[48:56, :] = jnp.where(taken, STEP * (step + 1), raw[48:56, :])

    def place_first():
        def one(n, _):
            at = pl.multiple_of(n * LANES, LANES)
            tiles = corr[:, pl.ds(at, LANES)]
            left[:, pl.ds(at, LANES)] = masked_pieces(0, at, tiles[0:8], tiles[8:16])
            return 0

        lax.fori_loop(0, chunks, one, 0, unroll=2)
        scat[...] = dot_nt(left[...], low_hot[0])
        settle(0)
        for n, v in enumerate(names):
            state_out[n, 0:1, :] = corr[v : v + 1, :]

    pick(0, src0)
    pl.semaphore_wait(barrier, len(partners))
    rs0 = scatter_picks(0)
    lay_field(0, rows0, value(raw, 7))
    f0, across0 = send_field(0)
    for n, row in enumerate(rows0):
        middle = jnp.sum(jnp.sum(row, axis=0, keepdims=True), axis=1, keepdims=True) / (8.0 * LANES)
        centre[n : n + 1, :] = jnp.broadcast_to(middle, (1, LANES))
    centre[6:8, :] = jnp.zeros((2, LANES), F32)
    pick(1, raw)
    build_low_hot(0)
    ar0 = reduce_picks(0, rs0)
    for dx in range(1, xs):
        pl.semaphore_signal(met, inc=1, device_id=device(0, 0, 0, dx), device_id_type=MESH)
    hit0 = hits(0)
    fresh[0] = hit0
    rows1, _ = predicted(2 * STEP)
    lay_field(1, rows1, jnp.where(hit0 > 0.5, 0.0, value(raw, 7)))
    pass_on(0, f0, across0)
    build_features(0, 0, zs * block)
    act0 = picked(0, ar0)
    rs1 = scatter_picks(1)
    f1, across1 = send_field(1)
    set_columns(act0)
    for copy in across0:
        copy.wait_recv()
    build_features(0, zs * block, 2 * zs * block)
    forces(0, act0, 2 * zs * block)
    early = len(started)
    s0 = send_sums(0)
    ar1 = reduce_picks(1, rs1)
    build_match()
    force0 = total_sums(0, s0)
    rows_a = correct(act0, force0)
    pl.semaphore_wait(met, xs - 1)
    next0 = gather_next(rows_a, act0[7:8])
    fresh0 = gather_fresh(0, rows_a)
    pass_on(1, f1, across1)
    build_low_hot(1)
    fresh[1] = hits(1)
    drain(early)
    act1_raw = picked(1, ar1)
    raw_high = swap(act1_raw)
    raw_elapsed = 2 * STEP - act1_raw[6:7]
    raw_pos, raw_vel = predict(
        act1_raw[0:3], act1_raw[3:6], raw_high[0:3], raw_high[3:6], raw_elapsed
    )
    for copy in across1:
        copy.wait_recv()
    build_features(1, 0, 2 * zs * block)
    by_chunks(next0, forward_next, take_next)

    extra = total // ys
    for n in range(extra // LANES):
        at = pl.multiple_of(y * extra + n * LANES, LANES)
        field[1, 2 * zs * block + n] = coming[:, pl.ds(at, LANES)]
    found = exact_nt(coming[...], match[...])
    found = jnp.concatenate([found, jnp.zeros((8, HALF), F32)], axis=1)
    again = found[7:8] > 0.5
    elapsed1 = jnp.where(again, 2 * STEP - STEP, raw_elapsed)
    ahead1 = jnp.where(again, found[0:6], jnp.concatenate([raw_pos, raw_vel], axis=0))
    low1 = jnp.concatenate([ahead1, elapsed1, act1_raw[7:8]], axis=0)
    set_columns(low1)
    build_features(1, 2 * zs * block, 2 * zs * block + extra // LANES)
    forces(1, low1, 2 * zs * block + extra // LANES)
    s1 = send_sums(1)
    by_chunks(fresh0, forward_fresh(0), take_fresh)
    held = jnp.concatenate([exact_nt(corr[8:16, :], match[...]), jnp.zeros((8, HALF), F32)], axis=1)
    act1 = pack(low1, jnp.where(again, held, raw_high))
    force1 = total_sums(1, s1)
    late = len(started)
    fresh1 = gather_fresh(1, correct(act1, force1))
    place_first()
    drain(late)
    by_chunks(fresh1, forward_fresh(1), take_last)
    scat[...] = dot_nt(left[...], low_hot[1])
    settle(1)
    for ref, at in ((pos_out, 0), (vel_out, 3), (acc_out, 8), (jerk_out, 11)):
        for comp in range(3):
            for hi in range(8):
                row = (at + comp) * 8 + hi
                ref[comp : comp + 1, hi * LANES : (hi + 1) * LANES] = raw[row : row + 1, :]
    time_out[...] = raw[48:56, :]
    drain(len(started))


def hand_on(*refs):
    srcs, dsts, sem = refs[0:6], refs[6:12], refs[12]
    stores = [pltpu.make_async_copy(a, b, sem.at[n]) for n, (a, b) in enumerate(zip(srcs, dsts))]
    for store in reversed(stores):
        store.start()
    for store in stores:
        store.wait()


def run(sizes, *args):
    zs, ys, xs = sizes
    total = xs * zs * LANES
    vmem = pltpu.VMEM
    dma = pltpu.SemaphoreType.DMA
    tiles = 2 * zs * 8 + total // ys // LANES
    scratch = [
        vmem((3, 1024), F32), vmem((3, 1024), F32), vmem((3, 1024), F32), vmem((3, 1024), F32),
        vmem((8, LANES), F32), vmem((8, LANES), F32), vmem((2, total), jnp.int32),
        vmem((112, LANES), F32), vmem((112, LANES), F32),
        vmem((2, zs, CORES, 8, LANES), F32), vmem((2, zs, CORES, 8, LANES), F32),
        vmem((2, 8, LANES), F32), vmem((2, ys, 8, LANES), F32),
        vmem((2, 8, LANES), F32), vmem((2, ys, 8, LANES), F32),
        vmem((2, tiles, 8, LANES), F32),
        vmem((2, CORES, zs, xs, 8, LANES), F32),
        vmem((6, HALF, LANES), F32), vmem((32, tiles * LANES), BF16), vmem((8, LANES), F32),
        vmem((16, total), F32), vmem((2, LANES, total), BF16), vmem((HALF, total), BF16),
        vmem((LANES, LANES), F32), vmem((288, LANES), F32), vmem((2, 8, LANES), F32),
        vmem((288, total), BF16),
        vmem((CORES, zs, xs, 4, LANES), F32), vmem((8, total), F32),
        dma((7,)),
        dma((2, zs, CORES)), dma((2, zs, CORES)),
        dma((2, ys)), dma((2, ys)), dma((2, ys)), dma((2, ys)),
        dma((2, zs)), dma((2, zs)), dma((2, zs)), dma((2, zs)),
        pltpu.SemaphoreType.REGULAR,
        dma((2, zs, xs)), dma((2, zs, xs)), dma((2, zs)), dma((2, zs)),
        dma((zs, xs)), dma((zs, xs)), dma((zs,)), dma((zs,)),
    ]
    flat = jax.ShapeDtypeStruct((3, 1024), F32)
    out_shape = [flat, flat, flat, flat, jax.ShapeDtypeStruct((8, LANES), F32),
                 jax.ShapeDtypeStruct((12, 2, total), F32)]
    args = [pltpu.with_memory_space_constraint(arg, pltpu.HBM) for arg in args]
    results = pl.pallas_call(
        functools.partial(kernel, sizes),
        out_shape=[pltpu.VMEM(out.shape, F32) for out in out_shape],
        in_specs=[pl.BlockSpec(memory_space=pltpu.HBM)] * 7,
        out_specs=[pl.BlockSpec(memory_space=pltpu.VMEM)] * 6,
        scratch_shapes=scratch,
        compiler_params=pltpu.CompilerParams(
            collective_id=0, has_side_effects=True, vmem_limit_bytes=40 << 20
        ),
        name="hermite",
    )(*args)
    return pl.pallas_call(
        hand_on,
        out_shape=out_shape,
        in_specs=[pl.BlockSpec(memory_space=pltpu.VMEM)] * 6,
        out_specs=[pl.BlockSpec(memory_space=pl.ANY)] * 6,
        scratch_shapes=[dma((6,))],
        compiler_params=pltpu.CompilerParams(vmem_limit_bytes=40 << 20),
        name="finish",
    )(*results)


def per_device(sizes, positions, velocities, accels, jerks, masses, last_time, active):
    pos, vel, acc, jerk, times, state = run(
        sizes, positions, velocities, accels, jerks,
        masses.reshape(8, LANES), last_time.reshape(8, LANES), active,
    )
    return pos, vel, acc, jerk, times.reshape(8 * LANES), state.transpose(1, 0, 2)


def solution(mesh, sizes=(RINGS["z"], RINGS["y"], RINGS["x"])):
    in_specs = (P(None, "ja"), P(None, "ja"), P(None, "ja"), P(None, "ja"), P("ja"), P("ja"), P())
    out_specs = (P(None, "ja"), P(None, "ja"), P(None, "ja"), P(None, "ja"), P("ja"), P())
    return jax.shard_map(
        functools.partial(per_device, sizes), mesh=mesh, in_specs=in_specs, out_specs=out_specs,
        check_vma=False,
    )
```
